32 devices in a mesh: wide: 4 (over z), row: 2 (over core), col: 4 (over y, x).
Axes of the slice: x: 2, y: 2, z: 4, core: 2. Of those that a mesh axis runs over, the one named last changes fastest.
Arguments:
- amplitudes: float32 [24, 256, 256], P('wide'), may hold values from -6 to 6
- factors: float32 [8, 512, 512], P(('row', 'col'), 'wide'), may hold values from -0.24 to 0.24
- domains: int32 [24, 4], P('wide'), may hold values from 0 to 7, as said below
- domain_mask: int32 [24, 4], P('wide'), may hold values 0 or 1
- block_mask: int32 [8, 8], replicated, may hold values 0 or 1
Outputs:
- ladder: float32 [24, 256, 256], P('wide', ('row', 'col'))
The draws below stay inside these ranges and needn't reach their ends.
Inputs may be any that keep to these rules, and one draw needn't show every extreme that they name: `domains`: each row names 4 different virtual blocks.
All inputs are finite; a program needn't handle non-finite values. No bound on the sum of `domain_mask` on one device may be relied on, other than what follows from the above.
Results may differ from the reference program's by a relative error of at most 0.0003.
Values sent between devices are 32-bit elements; how exact they have to be, the bound alone decides.
No kernel may reach another device: no remote copies, remote signals or barrier semaphores. Data moves between devices by JAX's collectives and lax.ppermute only.
A program may use at most 64 MiB of HBM per device.

```python
import jax
import jax.numpy as jnp
from jax import lax

BS = 64
DOM = 4
NBLK = 8
PAIRS = 24
DOMV = 256
V = 512
NAUX = 8


def draw_domains(key, part):
    key = jax.random.fold_in(key, 7)
    keys = jax.random.split(key, PAIRS)

    def one_row(row_key):
        return jax.random.permutation(row_key, NBLK)[:DOM]
    return jax.vmap(one_row)(keys).astype(jnp.int32)


def place_ends(values, key, least, high):
    longest = values.shape.index(max(values.shape))
    spots = []
    for shift in (0, 1):
        where = [jax.random.randint(jax.random.fold_in(key, axis), (), 0, length) for axis, length in enumerate(values.shape)]
        where[longest] = (where[longest] + shift) % values.shape[longest]
        spots.append(tuple(where))
    return values.at[spots[0]].set(least).at[spots[1]].set(high)


def shard_levels(stream_key, dims, shards, least, top_value):
    gain, own = 1.0, jax.random.fold_in(stream_key, 6)
    for dim, blocks in shards:
        heights = jnp.exp(jax.random.uniform(jax.random.fold_in(own, dim), (blocks,), jnp.float32, least / len(shards), top_value / len(shards)))
        gain = gain * jnp.repeat(heights, dims[dim] // blocks).reshape([-1 if axis == dim else 1 for axis in range(len(dims))])
    return gain


def normal_values(rng, extent, spread, reach, pieces=(), kind=jnp.bfloat16):
    entries = spread * jax.random.normal(rng, extent, jnp.float32)
    if pieces:
        entries = entries * shard_levels(rng, extent, pieces, -0.22, 0.18)
    return jnp.clip(entries, -reach, reach).astype(kind)


def setup_inputs(seed: int = 0) -> dict:
    seeds = jax.random.split(jax.random.key(seed), 6)
    return {
        "amplitudes": normal_values(seeds[0], (PAIRS, DOMV, DOMV), 1.0, 6.0, ((0, 4),), jnp.float32),
        "factors": normal_values(seeds[1], (NAUX, V, V), 0.04, 0.24, ((0, 8), (1, 4)), jnp.float32),
        "domains": draw_domains(jax.random.fold_in(seeds[5], 71), 0),
        "domain_mask": place_ends((jax.random.randint(seeds[3], (PAIRS, DOM), 0, 4) < 3).astype(jnp.int32), jax.random.fold_in(seeds[3], 1), 0, 1),
        "block_mask": place_ends((jax.random.randint(seeds[4], (NBLK, NBLK), 0, 4) < 3).astype(jnp.int32), jax.random.fold_in(seeds[4], 1), 0, 1),
    }


def contract_pair(tile, blocks, flags, screened):
    offsets = jnp.arange(BS, dtype=jnp.int32)
    indices = (blocks[:, None] * BS + offsets[None, :]).reshape(-1).astype(jnp.int32)
    weights = jnp.repeat(flags, BS).astype(jnp.float32)
    subset = screened[:, indices][:, :, indices]
    masked = tile * weights[:, None] * weights[None, :]
    halfway = jnp.einsum('qxu,uw->qxw', subset, masked, precision=lax.Precision.HIGHEST)
    result = jnp.einsum('qxw,qyw->xy', halfway, subset, precision=lax.Precision.HIGHEST)
    return result * weights[:, None] * weights[None, :]


def reference(amplitudes, factors, domains, domain_mask, block_mask):
    expanded = jnp.repeat(jnp.repeat(block_mask, BS, 0), BS, 1).astype(jnp.float32)
    screened = factors * expanded[None, :, :]

    def one_pair(items):
        return contract_pair(items[0], items[1], items[2], screened)

    return lax.map(one_pair, (amplitudes, domains, domain_mask))
```

```python
import functools

import jax
import jax.numpy as jnp
from jax import lax
from jax.experimental import pallas as pl
from jax.experimental.pallas import tpu as pltpu
from jax.sharding import PartitionSpec as P

BS = 64
LANES = 128
LINE = 4
VMEM_LIMIT = 40 * 1024 * 1024
SMEM_SPEC = pl.BlockSpec(memory_space=pltpu.SMEM)
VMEM_SPEC = pl.BlockSpec(memory_space=pltpu.VMEM)


def split(value):
    top = value.astype(jnp.bfloat16)
    return top, (value - top.astype(jnp.float32)).astype(jnp.bfloat16)


def pair_row(left_half, first, second):
    return jnp.where(left_half, first.astype(jnp.float32), second.astype(jnp.float32))


def left_of(rows):
    return lax.broadcasted_iota(jnp.int32, (rows, LANES), 1) < BS


def mask_amplitudes_kernel(flags, amplitudes, high, low):
    pairs, domv, _ = amplitudes.shape
    left_half = left_of(1)
    for p in range(pairs):
        for j in range(domv // LANES):
            row = pair_row(left_half, flags[2 * j, p], flags[2 * j + 1, p])
            lanes = slice(j * LANES, (j + 1) * LANES)
            for i in range(domv // BS):
                rows = slice(i * BS, (i + 1) * BS)
                top, rest = split(amplitudes[p, rows, lanes] * (row * flags[i, p].astype(jnp.float32)))
                high[p, rows, lanes] = top
                low[p, rows, lanes] = rest


def mask_amplitudes(flags, amplitudes):
    shape = jax.ShapeDtypeStruct(amplitudes.shape, jnp.bfloat16)
    return pl.pallas_call(
        mask_amplitudes_kernel,
        name="mask_amplitudes",
        out_shape=[shape] * 2,
        in_specs=[SMEM_SPEC, VMEM_SPEC],
        out_specs=[VMEM_SPEC] * 2,
        compiler_params=pltpu.CompilerParams(vmem_limit_bytes=VMEM_LIMIT),
        cost_estimate=pl.CostEstimate(flops=4 * amplitudes.size, bytes_accessed=8 * amplitudes.size, transcendentals=0),
    )(flags, amplitudes)


def screen_piece(place, block_mask, piece, q, slot, high, low):
    nq, rows, window = piece.shape
    tiles = window // LANES
    per_slot = rows // BS
    left_half = left_of(1)
    for h in range(per_slot):
        block = (place[0] ^ slot) * per_slot + h
        for t in range(tiles):
            row = pair_row(left_half, block_mask[block, 2 * t], block_mask[block, 2 * t + 1])
            for n in range(nq):
                tile = piece[n, h * BS:(h + 1) * BS, t * LANES:(t + 1) * LANES] * row
                target = pl.ds(pl.multiple_of(slot * rows + h * BS, BS), BS)
                for turn, value in ((0, tile), (1, pltpu.roll(tile, BS, 1))):
                    top, rest = split(value)
                    high[turn * tiles + t, q * nq + n, target, :] = top
                    low[turn * tiles + t, q * nq + n, target, :] = rest


def screen_kernel(keys, place, block_mask, *refs):
    high, low = refs[-2:]
    for (slots, q), pieces in zip(keys, refs):
        for i, slot in enumerate(slots):
            if slot is not None:
                screen_piece(place, block_mask, pieces.at[i], q, slot, high, low)


def screen(place, block_mask, keyed, shape, held=()):
    keys = [(slots, q) for slots, q, _ in keyed]
    pieces = [piece for _, _, piece in keyed]
    size = sum(piece.size for piece in pieces)
    return pl.pallas_call(
        functools.partial(screen_kernel, keys),
        name="screen_factors",
        out_shape=[shape] * 2,
        in_specs=[SMEM_SPEC] * 2 + [VMEM_SPEC] * (len(pieces) + len(held)),
        out_specs=[VMEM_SPEC] * 2,
        input_output_aliases={2 + len(pieces) + i: i for i in range(len(held))},
        compiler_params=pltpu.CompilerParams(vmem_limit_bytes=VMEM_LIMIT),
        cost_estimate=pl.CostEstimate(flops=8 * size, bytes_accessed=12 * size, transcendentals=0),
    )(place, block_mask, *pieces, *held)


def collect_kernel(place, near, mid, crossed, second, far, stack):
    middle = (place[0] > 0) & (place[0] < LINE - 1)
    stack[0] = near[...]

    @pl.when(middle)
    def _():
        stack[1] = crossed[...]
        stack[2] = mid[...]

    @pl.when(jnp.logical_not(middle))
    def _():
        stack[1] = second[...]
        stack[2] = far[...]


def collect(place, near, *received):
    return pl.pallas_call(
        collect_kernel,
        name="collect_pieces",
        out_shape=jax.ShapeDtypeStruct((LINE - 1,) + near.shape, near.dtype),
        in_specs=[SMEM_SPEC] + [VMEM_SPEC] * 5,
        out_specs=VMEM_SPEC,
        compiler_params=pltpu.CompilerParams(vmem_limit_bytes=VMEM_LIMIT),
        cost_estimate=pl.CostEstimate(flops=0, bytes_accessed=2 * (LINE - 1) * near.size * 4, transcendentals=0),
    )(place, near, *received)


def pairs_kernel(row, line, late, place, block_mask, domains, flags, *refs):
    pieces = refs[:len(late)]
    mhigh, mlow, _, _ = refs[len(late):len(late) + 4]
    out, high, low, yhigh, ylow = refs[len(late) + 4:]
    z, r = place[0], place[1]
    for q, piece in zip(late, pieces):

        @pl.loop(1, line)
        def _(slot):
            screen_piece(place, block_mask, piece.at[slot - 1], q, slot, high, low)

    col, pairs, chunk, domv = out.shape
    twice, qs, window, _ = high.shape
    tiles = twice // 2
    rows = window // line
    per_slot = rows // BS
    half = domv // row
    left_half = left_of(BS)
    picks = [r * half + k * chunk for k in range(col)]
    across = (((1,), (1,)), ((), ()))
    dot = functools.partial(lax.dot_general, preferred_element_type=jnp.float32)
    along = (((1,), (0,)), ((), ()))
    for p in range(pairs):
        slot = p % 2
        spans = []
        for i in range(domv // BS):
            block = domains[i, p]
            start = ((block // per_slot) ^ z) * rows + (block % per_slot) * BS
            spans.append(pl.ds(pl.multiple_of(start, BS), BS))
        sources = []
        for j in range(domv // LANES):
            first, second = domains[2 * j, p], domains[2 * j + 1, p]
            from_first = (first % 2) * tiles + first // 2
            from_second = (1 - second % 2) * tiles + second // 2
            sources.append((from_first, from_second))
            for i, span in enumerate(spans):
                for q in range(qs):
                    lanes = slice(q * domv + j * LANES, q * domv + (j + 1) * LANES)
                    for source, target in ((high, yhigh), (low, ylow)):
                        target[slot, i * BS:(i + 1) * BS, lanes] = jnp.where(
                            left_half, source[from_first, q, span, :], source[from_second, q, span, :])
        xs = []
        for source in (high, low):
            rows_of = []
            for q in range(qs):
                for pick in picks:
                    block = domains[pick // BS, p]
                    start = ((block // per_slot) ^ z) * rows + (block % per_slot) * BS + pick % BS
                    span = pl.ds(pl.multiple_of(start, chunk), chunk)
                    rows_of.append(jnp.concatenate([jnp.where(
                        left_of(chunk), source[a, q, span, :], source[b, q, span, :]) for a, b in sources], 1))
            xs.append(jnp.concatenate(rows_of, 0))
        xhigh, xlow = xs
        halfway = dot(xhigh, mhigh[p], along) + dot(xhigh, mlow[p], along) + dot(xlow, mhigh[p], along)
        hhigh, hlow = split(jnp.concatenate([halfway[q * half:(q + 1) * half] for q in range(qs)], 1))
        total = (dot(hhigh, yhigh[slot], across) + dot(hhigh, ylow[slot], across) + dot(hlow, yhigh[slot], across))
        for j in range(domv // LANES):
            weights = pair_row(left_of(1), flags[2 * j, p], flags[2 * j + 1, p])
            for k, pick in enumerate(picks):
                weight = flags[pick // BS, p].astype(jnp.float32)
                out[k, p, :, j * LANES:(j + 1) * LANES] = total[
                    k * chunk:(k + 1) * chunk, j * LANES:(j + 1) * LANES] * (weights * weight)


def contract_pairs(row, col, line, place, block_mask, domains, flags, late, mhigh, mlow, high, low):
    pairs, domv, _ = mhigh.shape
    chunk = domv // (row * col)
    qs = high.shape[1]
    order = range(1, len(late) + 1)
    first = 4 + len(late) + 2
    shape = jax.ShapeDtypeStruct((col, pairs, chunk, domv), jnp.float32)
    terms, _, _ = pl.pallas_call(
        functools.partial(pairs_kernel, row, line, order),
        name="contract_pairs",
        out_shape=[shape] + [jax.ShapeDtypeStruct(high.shape, high.dtype)] * 2,
        in_specs=[SMEM_SPEC] * 4 + [VMEM_SPEC] * (len(late) + 4),
        out_specs=[VMEM_SPEC] * 3,
        scratch_shapes=[pltpu.VMEM((2, domv, qs * domv), jnp.bfloat16)] * 2,
        input_output_aliases={first: 1, first + 1: 2},
        compiler_params=pltpu.CompilerParams(vmem_limit_bytes=VMEM_LIMIT),
        cost_estimate=pl.CostEstimate(flops=6 * pairs * qs * domv ** 3 * 4 // row, bytes_accessed=8 * high.size,
                                      transcendentals=0),
    )(place, block_mask, domains, flags, *late, mhigh, mlow, high, low)
    return terms


def body(wide, row, col, amplitudes, factors, domains, domain_mask, block_mask):
    nq, rows, window = factors.shape
    z, r, c = lax.axis_index("wide"), lax.axis_index("row"), lax.axis_index("col")
    shape = jax.ShapeDtypeStruct((2 * window // LANES, row * nq, window, LANES), jnp.bfloat16)
    domains, flags = domains.T, domain_mask.T
    mhigh, mlow = mask_amplitudes(flags, amplitudes)

    def siblings(piece):
        return [lax.ppermute(piece, "row", [(i, (i + s) % row) for i in range(row)]) for s in range(1, row)]

    if wide == LINE and rows % BS == 0:
        line = wide
        place = jnp.stack([z, r, c]).astype(jnp.int32)
        near = lax.ppermute(factors, "wide", [(0, 1), (1, 0), (2, 3), (3, 2)])
        mid = lax.ppermute(factors, "wide", [(1, 2), (2, 1)])
        crossed = lax.ppermute(near, "wide", [(1, 2), (2, 1)])
        second = lax.ppermute(mid, "wide", [(1, 0), (2, 3)])
        far = lax.ppermute(near, "wide", [(1, 3), (2, 0)])
        early = [((0,), q, piece[None]) for q, piece in enumerate([factors] + siblings(factors))]
        early += [((1,), 0, near[None]), ((3,), 0, mid[None])]
        high, low = screen(place, block_mask, early, shape)
        second, crossed, far, high, low, mhigh, mlow, domains = lax.optimization_barrier(
            (second, crossed, far, high, low, mhigh, mlow, domains))
        stack = collect(place, near, mid, crossed, second, far)
        late = siblings(stack)
        high, low = screen(place, block_mask, [((None, 2, 3), 0, stack)], shape, (high, low))
    else:
        line = 1
        place = jnp.stack([jnp.zeros_like(z), r, c]).astype(jnp.int32)
        whole = lax.all_gather(factors, "wide", axis=1, tiled=True)
        high, low = screen(place, block_mask, [((0,), q, piece[None]) for q, piece in enumerate([whole] + siblings(whole))], shape)
        late = []

    terms = contract_pairs(row, col, line, place, block_mask, domains, flags, late, mhigh, mlow, high, low)
    return jnp.sum(lax.all_to_all(terms, "col", 0, 0, tiled=True), axis=0)


def solution(mesh):
    wide, row, col = (mesh.shape[name] for name in ("wide", "row", "col"))
    return jax.shard_map(
        functools.partial(body, wide, row, col),
        mesh=mesh,
        in_specs=(
            P("wide", None, None),
            P(("row", "col"), "wide", None),
            P("wide", None),
            P("wide", None),
            P(),
        ),
        out_specs=P("wide", ("row", "col"), None),
        check_vma=False,
    )
```

```python
import functools

import jax
import jax.numpy as jnp
from jax import lax
from jax.experimental import pallas as pl
from jax.experimental.pallas import tpu as pltpu
from jax.sharding import PartitionSpec as P

BS = 64
LANES = 128
LINE = 4
SLOTS = 3
VMEM_LIMIT = 40 * 1024 * 1024
SMEM_SPEC = pl.BlockSpec(memory_space=pltpu.SMEM)
VMEM_SPEC = pl.BlockSpec(memory_space=pltpu.VMEM)


def split(value):
    top = value.astype(jnp.bfloat16)
    return top, (value - top.astype(jnp.float32)).astype(jnp.bfloat16)


def partner(index, shift, size):
    if size & (size - 1) == 0:
        return index ^ shift
    return (index + shift) % size


def pair_row(left_half, first, second):
    return jnp.where(left_half, first.astype(jnp.float32), second.astype(jnp.float32))


def left_of(rows):
    return lax.broadcasted_iota(jnp.int32, (rows, LANES), 1) < BS


def mask_amplitudes_kernel(flags, amplitudes, high, low):
    pairs, domv, _ = amplitudes.shape
    left_half = left_of(1)
    for p in range(pairs):
        for j in range(domv // LANES):
            row = pair_row(left_half, flags[2 * j, p], flags[2 * j + 1, p])
            lanes = slice(j * LANES, (j + 1) * LANES)
            for i in range(domv // BS):
                rows = slice(i * BS, (i + 1) * BS)
                top, rest = split(amplitudes[p, rows, lanes] * (row * flags[i, p].astype(jnp.float32)))
                high[p, rows, lanes] = top
                low[p, rows, lanes] = rest


def mask_amplitudes(flags, amplitudes):
    shape = jax.ShapeDtypeStruct(amplitudes.shape, jnp.bfloat16)
    return pl.pallas_call(
        mask_amplitudes_kernel,
        name="mask_amplitudes",
        out_shape=[shape] * 2,
        in_specs=[SMEM_SPEC, VMEM_SPEC],
        out_specs=[VMEM_SPEC] * 2,
        compiler_params=pltpu.CompilerParams(vmem_limit_bytes=VMEM_LIMIT),
        cost_estimate=pl.CostEstimate(flops=4 * amplitudes.size, bytes_accessed=8 * amplitudes.size, transcendentals=0),
    )(flags, amplitudes)


def screen_piece(place, block_mask, piece, q, slot, high, low):
    nq, rows, window = piece.shape
    tiles = window // LANES
    per_slot = rows // BS
    left_half = left_of(1)
    for h in range(per_slot):
        block = (place[0] ^ slot) * per_slot + h
        for t in range(tiles):
            row = pair_row(left_half, block_mask[block, 2 * t], block_mask[block, 2 * t + 1])
            for n in range(nq):
                tile = piece[n, h * BS:(h + 1) * BS, t * LANES:(t + 1) * LANES] * row
                target = pl.ds(pl.multiple_of(slot * rows + h * BS, BS), BS)
                for turn, value in ((0, tile), (1, pltpu.roll(tile, BS, 1))):
                    top, rest = split(value)
                    high[turn * tiles + t, q * nq + n, target, :] = top
                    low[turn * tiles + t, q * nq + n, target, :] = rest


def screen_kernel(keys, place, block_mask, *refs):
    high, low = refs[-2:]
    for (slots, q), pieces in zip(keys, refs):
        for i, slot in enumerate(slots):
            if slot is not None:
                screen_piece(place, block_mask, pieces.at[i], q, slot, high, low)


def screen(place, block_mask, keyed, shape, held=()):
    keys = [(slots, q) for slots, q, _ in keyed]
    pieces = [piece for _, _, piece in keyed]
    size = sum(piece.size for piece in pieces)
    return pl.pallas_call(
        functools.partial(screen_kernel, keys),
        name="screen_factors",
        out_shape=[shape] * 2,
        in_specs=[SMEM_SPEC] * 2 + [VMEM_SPEC] * (len(pieces) + len(held)),
        out_specs=[VMEM_SPEC] * 2,
        input_output_aliases={2 + len(pieces) + i: i for i in range(len(held))},
        compiler_params=pltpu.CompilerParams(vmem_limit_bytes=VMEM_LIMIT),
        cost_estimate=pl.CostEstimate(flops=8 * size, bytes_accessed=12 * size, transcendentals=0),
    )(place, block_mask, *pieces, *held)


def pairs_kernel(row, line, layout, late, place, block_mask, domains, flags, *refs):
    pieces = refs[:len(late)]
    mhigh, mlow, _, _ = refs[len(late):len(late) + 4]
    outs = refs[len(late) + 4:len(late) + 4 + len(layout)]
    high, low, xhigh, xlow, hhigh, hlow, yhigh, ylow = refs[len(late) + 4 + len(layout):]
    z, r = place[0], place[1]
    for (slot, q), piece in zip(late, pieces):

        @pl.loop(slot, slot + 1)
        def _(n):
            screen_piece(place, block_mask, piece, q, n, high, low)

    _, pairs, chunk, domv = outs[0].shape
    twice, qs, window, _ = high.shape
    tiles = twice // 2
    rows = window // line
    per_slot = rows // BS
    half = domv // row
    left_half = left_of(BS)
    picks = [r * half + place[at] * chunk for part in layout for at in part]
    targets = [out.at[i] for out, part in zip(outs, layout) for i in range(len(part))]
    across = (((1,), (1,)), ((), ()))
    dot = functools.partial(lax.dot_general, preferred_element_type=jnp.float32)
    along = (((1,), (0,)), ((), ()))

    def gather(p):
        spans = []
        for i in range(domv // BS):
            block = domains[i, p]
            start = ((block // per_slot) ^ z) * rows + (block % per_slot) * BS
            spans.append(pl.ds(pl.multiple_of(start, BS), BS))
        sources = []
        for j in range(domv // LANES):
            first, second = domains[2 * j, p], domains[2 * j + 1, p]
            sources.append(((first % 2) * tiles + first // 2, (1 - second % 2) * tiles + second // 2))
        for source, target in ((high, yhigh), (low, ylow)):
            for j, (a, b) in enumerate(sources):
                for i, span in enumerate(spans):
                    for q in range(qs):
                        lanes = slice(q * domv + j * LANES, q * domv + (j + 1) * LANES)
                        target[p % SLOTS, i * BS:(i + 1) * BS, lanes] = jnp.where(
                            left_half, source[a, q, span, :], source[b, q, span, :])
        for source, target in ((high, xhigh), (low, xlow)):
            for q in range(qs):
                for n, pick in enumerate(picks):
                    block = domains[pick // BS, p]
                    start = ((block // per_slot) ^ z) * rows + (block % per_slot) * BS + pick % BS
                    span = pl.ds(pl.multiple_of(start, chunk), chunk)
                    for j, (a, b) in enumerate(sources):
                        target[p % SLOTS, q * half + n * chunk:q * half + (n + 1) * chunk, j * LANES:(j + 1) * LANES] = (
                            jnp.where(left_of(chunk), source[a, q, span, :], source[b, q, span, :]))

    def first_product(p):
        at = p % SLOTS
        halfway = dot(xhigh[at], mhigh[p], along) + dot(xhigh[at], mlow[p], along) + dot(xlow[at], mhigh[p], along)
        for q in range(qs):
            top, rest = split(halfway[q * half:(q + 1) * half])
            hhigh[at, :, q * domv:(q + 1) * domv] = top
            hlow[at, :, q * domv:(q + 1) * domv] = rest

    def second_product(p):
        at = p % SLOTS
        total = (dot(hhigh[at], yhigh[at], across) + dot(hhigh[at], ylow[at], across)
                 + dot(hlow[at], yhigh[at], across))
        for j in range(domv // LANES):
            weights = pair_row(left_of(1), flags[2 * j, p], flags[2 * j + 1, p])
            for n, (pick, target) in enumerate(zip(picks, targets)):
                weight = flags[pick // BS, p].astype(jnp.float32)
                target[p, :, j * LANES:(j + 1) * LANES] = total[
                    n * chunk:(n + 1) * chunk, j * LANES:(j + 1) * LANES] * (weights * weight)

    for t in range(pairs + 2):
        for stage, act in ((0, gather), (1, first_product), (2, second_product)):
            if 0 <= t - stage < pairs:
                act(t - stage)


def contract_pairs(row, line, layout, place, block_mask, domains, flags, late, mhigh, mlow, high, low):
    pairs, domv, _ = mhigh.shape
    chunk = domv // (row * sum(len(part) for part in layout))
    qs = high.shape[1]
    keys = [(slot, q) for slot, q, _ in late]
    pieces = [piece for _, _, piece in late]
    held = 4 + len(pieces) + 2
    outs = len(layout)
    results = pl.pallas_call(
        functools.partial(pairs_kernel, row, line, layout, keys),
        name="contract_pairs",
        out_shape=[jax.ShapeDtypeStruct((len(part), pairs, chunk, domv), jnp.float32) for part in layout]
        + [jax.ShapeDtypeStruct(high.shape, high.dtype)] * 2,
        in_specs=[SMEM_SPEC] * 4 + [VMEM_SPEC] * (len(pieces) + 4),
        out_specs=[VMEM_SPEC] * (outs + 2),
        scratch_shapes=[pltpu.VMEM((SLOTS, qs * domv // row, domv), jnp.bfloat16)] * 2
        + [pltpu.VMEM((SLOTS, domv // row, qs * domv), jnp.bfloat16)] * 2
        + [pltpu.VMEM((SLOTS, domv, qs * domv), jnp.bfloat16)] * 2,
        input_output_aliases={held: outs, held + 1: outs + 1},
        compiler_params=pltpu.CompilerParams(vmem_limit_bytes=VMEM_LIMIT),
        cost_estimate=pl.CostEstimate(flops=6 * pairs * qs * domv ** 3 * 4 // row, bytes_accessed=8 * high.size,
                                      transcendentals=0),
    )(place, block_mask, domains, flags, *pieces, mhigh, mlow, high, low)
    return results[:outs]


def add_kernel(at, *refs):
    out = refs[-1]
    total = refs[0][at[0]]
    for i, ref in zip(at[1:], refs[1:]):
        total += ref[i]
    out[...] = total


def add_terms(*terms):
    arrays = [array for array, _ in terms]
    return pl.pallas_call(
        functools.partial(add_kernel, [i for _, i in terms]),
        name="add_terms",
        out_shape=jax.ShapeDtypeStruct(arrays[0].shape[1:], jnp.float32),
        in_specs=[VMEM_SPEC] * len(arrays),
        out_specs=VMEM_SPEC,
        compiler_params=pltpu.CompilerParams(vmem_limit_bytes=VMEM_LIMIT),
    )(*arrays)


def body(wide, row, col, amplitudes, factors, domains, domain_mask, block_mask):
    nq, rows, window = factors.shape
    pairs = domains.shape[0]
    z, r, c = lax.axis_index("wide"), lax.axis_index("row"), lax.axis_index("col")
    shape = jax.ShapeDtypeStruct((2 * window // LANES, row * nq, window, LANES), jnp.bfloat16)
    domains, flags = domains.T, domain_mask.T
    mhigh, mlow = mask_amplitudes(flags, amplitudes)

    def siblings(piece):
        return [lax.ppermute(piece, "row", [(i, (i + s) % row) for i in range(row)]) for s in range(1, row)]

    layout = tuple((2 + s,) for s in range(col))
    chunks = [partner(c, s, col) for s in range(col)]

    if wide == LINE and rows % BS == 0:
        line = wide
        place = jnp.stack([z, r] + chunks).astype(jnp.int32)
        near = lax.ppermute(factors, "wide", [(i, i ^ 1) for i in range(line)])
        cross = lax.ppermute(factors, "wide", [(i, i ^ 2) for i in range(line)])
        high, low = screen(place, block_mask, [((0,), 0, factors[None])], shape)
        cross, high, low, mhigh, mlow, domains = lax.optimization_barrier((cross, high, low, mhigh, mlow, domains))
        last = lax.ppermute(cross, "wide", [(i, i ^ 1) for i in range(line)])
        early = [((0,), q + 1, piece[None]) for q, piece in enumerate(siblings(factors))]
        early += [((1,), 0, near[None]), ((2,), 0, cross[None])]
        high, low = screen(place, block_mask, early, shape, (high, low))
        last, cross, near, high, low = lax.optimization_barrier((last, siblings(cross), siblings(near), high, low))
        late = [(3, q + 1, piece) for q, piece in enumerate(siblings(last))]
        held = [((3,), 0, last[None])]
        for slot, pieces in ((1, near), (2, cross)):
            held += [((slot,), q + 1, piece[None]) for q, piece in enumerate(pieces)]
        high, low = screen(place, block_mask, held, shape, (high, low))
    else:
        line = 1
        place = jnp.stack([jnp.zeros_like(z), r] + chunks).astype(jnp.int32)
        whole = lax.all_gather(factors, "wide", axis=1, tiled=True)
        held = [((0,), q, piece[None]) for q, piece in enumerate([whole] + siblings(whole))]
        high, low = screen(place, block_mask, held, shape)
        late = []

    terms = contract_pairs(row, line, layout, place, block_mask, domains, flags, late, mhigh, mlow, high, low)
    moved = [(lax.ppermute(terms[s], "col", [(i, partner(i, s, col)) for i in range(col)]), 0)
             for s in sorted(range(1, col), key=lambda s: -bin(s).count("1"))]
    return add_terms((terms[0], 0), *moved)


def solution(mesh):
    wide, row, col = (mesh.shape[name] for name in ("wide", "row", "col"))
    return jax.shard_map(
        functools.partial(body, wide, row, col),
        mesh=mesh,
        in_specs=(
            P("wide", None, None),
            P(("row", "col"), "wide", None),
            P("wide", None),
            P("wide", None),
            P(),
        ),
        out_specs=P("wide", ("row", "col"), None),
        check_vma=False,
    )
```

```python
import functools

import jax
import jax.numpy as jnp
from jax import lax
from jax.experimental import pallas as pl
from jax.experimental.pallas import tpu as pltpu
from jax.sharding import PartitionSpec as P

BS = 64
LANES = 128
LINE = 4
VMEM_LIMIT = 40 * 1024 * 1024
SMEM_SPEC = pl.BlockSpec(memory_space=pltpu.SMEM)
VMEM_SPEC = pl.BlockSpec(memory_space=pltpu.VMEM)


def split(value):
    top = value.astype(jnp.bfloat16)
    return top, (value - top.astype(jnp.float32)).astype(jnp.bfloat16)


def partner(index, shift, size):
    if size & (size - 1) == 0:
        return index ^ shift
    return (index + shift) % size


def left_of(rows):
    return lax.broadcasted_iota(jnp.int32, (rows, LANES), 1) < BS


class Scalars:
    def __init__(self, info, col, pairs, dom, blocks):
        self.info, self.pairs, self.blocks = info, pairs, blocks
        self.domains = 2 + col
        self.flags = self.domains + dom * pairs
        self.mask = self.flags + dom * pairs

    def place(self, at):
        return self.info[at]

    def domain(self, at, pair):
        return self.info[self.domains + at * self.pairs + pair]

    def flag(self, at, pair):
        return self.info[self.flags + at * self.pairs + pair].astype(jnp.float32)

    def kept(self, first, second):
        return self.info[self.mask + first * self.blocks + second].astype(jnp.float32)


def mask_amplitudes_kernel(read, info, amplitudes, high, low):
    scalars = read(info)
    pairs, domv, _ = amplitudes.shape
    left_half = left_of(1)

    @pl.loop(0, pairs)
    def _(p):
        for j in range(domv // LANES):
            row = jnp.where(left_half, scalars.flag(2 * j, p), scalars.flag(2 * j + 1, p))
            lanes = slice(j * LANES, (j + 1) * LANES)
            for i in range(domv // BS):
                rows = slice(i * BS, (i + 1) * BS)
                top, rest = split(amplitudes[p, rows, lanes] * (row * scalars.flag(i, p)))
                high[p, rows, lanes] = top
                low[p, rows, lanes] = rest


def mask_amplitudes(read, info, amplitudes):
    shape = jax.ShapeDtypeStruct(amplitudes.shape, jnp.bfloat16)
    return pl.pallas_call(
        functools.partial(mask_amplitudes_kernel, read),
        name="mask_amplitudes",
        out_shape=[shape] * 2,
        in_specs=[SMEM_SPEC, VMEM_SPEC],
        out_specs=[VMEM_SPEC] * 2,
        compiler_params=pltpu.CompilerParams(vmem_limit_bytes=VMEM_LIMIT),
        cost_estimate=pl.CostEstimate(flops=4 * amplitudes.size, bytes_accessed=8 * amplitudes.size, transcendentals=0),
    )(info, amplitudes)


def screen_piece(scalars, piece, q, slot, high, low):
    nq, rows, window = piece.shape
    tiles = window // LANES
    per_slot = rows // BS
    left_half = left_of(1)

    @pl.loop(0, tiles)
    def _(t):
        lanes = pl.ds(pl.multiple_of(t * LANES, LANES), LANES)
        for h in range(per_slot):
            block = (scalars.place(0) ^ slot) * per_slot + h
            row = jnp.where(left_half, scalars.kept(block, 2 * t), scalars.kept(block, 2 * t + 1))
            target = slice(slot * rows + h * BS, slot * rows + (h + 1) * BS)
            for n in range(nq):
                tile = piece[n, h * BS:(h + 1) * BS, lanes] * row
                for turn, value in ((0, tile), (1, pltpu.roll(tile, BS, 1))):
                    top, rest = split(value)
                    high[turn * tiles + t, q * nq + n, target, :] = top
                    low[turn * tiles + t, q * nq + n, target, :] = rest


def screen_kernel(read, keys, info, *refs):
    high, low = refs[-2:]
    for (slot, q), piece in zip(keys, refs):
        screen_piece(read(info), piece, q, slot, high, low)


def screen(read, info, keyed, shape, held=()):
    keys = [(slot, q) for slot, q, _ in keyed]
    pieces = [piece for _, _, piece in keyed]
    size = sum(piece.size for piece in pieces)
    return pl.pallas_call(
        functools.partial(screen_kernel, read, keys),
        name="screen_factors",
        out_shape=[shape] * 2,
        in_specs=[SMEM_SPEC] + [VMEM_SPEC] * (len(pieces) + len(held)),
        out_specs=[VMEM_SPEC] * 2,
        input_output_aliases={1 + len(pieces) + i: i for i in range(len(held))},
        compiler_params=pltpu.CompilerParams(vmem_limit_bytes=VMEM_LIMIT),
        cost_estimate=pl.CostEstimate(flops=8 * size, bytes_accessed=12 * size, transcendentals=0),
    )(info, *pieces, *held)


def pairs_kernel(read, row, line, late, info, *refs):
    scalars = read(info)
    pieces = refs[:len(late)]
    mhigh, mlow, _, _ = refs[len(late):len(late) + 4]
    outs = refs[len(late) + 4:-4]
    high, low, yhigh, ylow = refs[-4:]
    z, r = scalars.place(0), scalars.place(1)
    for (slot, q), piece in zip(late, pieces):
        screen_piece(scalars, piece, q, slot, high, low)

    pairs, chunk, domv = outs[0].shape
    twice, qs, window, _ = high.shape
    tiles = twice // 2
    rows = window // line
    per_slot = rows // BS
    half = domv // row
    picks = [r * half + scalars.place(2 + s) * chunk for s in range(len(outs))]
    across = (((1,), (1,)), ((), ()))
    along = (((1,), (0,)), ((), ()))
    dot = functools.partial(lax.dot_general, preferred_element_type=jnp.float32)

    @pl.loop(0, pairs)
    def _(p):
        def rows_of(at, offset, size):
            block = scalars.domain(at, p)
            start = ((block // per_slot) ^ z) * rows + (block % per_slot) * BS + offset
            return pl.ds(pl.multiple_of(start, size), size)

        sources = []
        for j in range(domv // LANES):
            first, second = scalars.domain(2 * j, p), scalars.domain(2 * j + 1, p)
            sources.append(((first % 2) * tiles + first // 2, (1 - second % 2) * tiles + second // 2))
        spans = [rows_of(i, 0, BS) for i in range(domv // BS)]
        xs = []
        for source, target in ((high, yhigh), (low, ylow)):
            for j, (a, b) in enumerate(sources):
                for i, span in enumerate(spans):
                    for q in range(qs):
                        lanes = slice(q * domv + j * LANES, q * domv + (j + 1) * LANES)
                        target[i * BS:(i + 1) * BS, lanes] = jnp.where(
                            left_of(BS), source[a, q, span, :], source[b, q, span, :])
            parts = []
            for q in range(qs):
                for pick in picks:
                    span = rows_of(pick // BS, pick % BS, chunk)
                    parts.append(jnp.concatenate([jnp.where(
                        left_of(chunk), source[a, q, span, :], source[b, q, span, :]) for a, b in sources], 1))
            xs.append(jnp.concatenate(parts, 0))
        xhigh, xlow = xs
        halfway = dot(xhigh, mhigh[p], along) + dot(xhigh, mlow[p], along) + dot(xlow, mhigh[p], along)
        hhigh, hlow = split(jnp.concatenate([halfway[q * half:(q + 1) * half] for q in range(qs)], 1))
        total = dot(hhigh, yhigh[...], across) + dot(hhigh, ylow[...], across) + dot(hlow, yhigh[...], across)
        for j in range(domv // LANES):
            weights = jnp.where(left_of(1), scalars.flag(2 * j, p), scalars.flag(2 * j + 1, p))
            for n, (pick, out) in enumerate(zip(picks, outs)):
                out[p, :, j * LANES:(j + 1) * LANES] = total[
                    n * chunk:(n + 1) * chunk, j * LANES:(j + 1) * LANES] * (weights * scalars.flag(pick // BS, p))


def contract_pairs(read, row, col, line, info, late, mhigh, mlow, high, low):
    pairs, domv, _ = mhigh.shape
    chunk = domv // (row * col)
    qs = high.shape[1]
    keys = [(slot, q) for slot, q, _ in late]
    pieces = [piece for _, _, piece in late]
    held = 1 + len(pieces) + 2
    results = pl.pallas_call(
        functools.partial(pairs_kernel, read, row, line, keys),
        name="contract_pairs",
        out_shape=[jax.ShapeDtypeStruct((pairs, chunk, domv), jnp.float32)] * col
        + [jax.ShapeDtypeStruct(high.shape, high.dtype)] * 2,
        in_specs=[SMEM_SPEC] + [VMEM_SPEC] * (len(pieces) + 4),
        out_specs=[VMEM_SPEC] * (col + 2),
        scratch_shapes=[pltpu.VMEM((domv, qs * domv), jnp.bfloat16)] * 2,
        input_output_aliases={held: col, held + 1: col + 1},
        compiler_params=pltpu.CompilerParams(vmem_limit_bytes=VMEM_LIMIT),
        cost_estimate=pl.CostEstimate(flops=6 * pairs * qs * domv ** 3 * 4 // row, bytes_accessed=8 * high.size,
                                      transcendentals=0),
    )(info, *pieces, mhigh, mlow, high, low)
    return results[:col]


def add_kernel(*refs):
    total = refs[0][...]
    for ref in refs[1:-1]:
        total += ref[...]
    refs[-1][...] = total


def add_terms(*terms):
    return pl.pallas_call(
        add_kernel,
        name="add_terms",
        out_shape=jax.ShapeDtypeStruct(terms[0].shape, jnp.float32),
        in_specs=[VMEM_SPEC] * len(terms),
        out_specs=VMEM_SPEC,
        compiler_params=pltpu.CompilerParams(vmem_limit_bytes=VMEM_LIMIT),
    )(*terms)


def body(wide, row, col, amplitudes, factors, domains, domain_mask, block_mask):
    nq, rows, window = factors.shape
    pairs, dom = domains.shape
    z, r, c = lax.axis_index("wide"), lax.axis_index("row"), lax.axis_index("col")
    line = wide if wide == LINE and rows % BS == 0 else 1
    place = jnp.stack([z if line > 1 else jnp.zeros_like(z), r] + [partner(c, s, col) for s in range(col)])
    info = jnp.concatenate([place.astype(jnp.int32), domains.T.reshape(-1), domain_mask.T.reshape(-1), block_mask.reshape(-1)])

    def read(ref):
        return Scalars(ref, col, pairs, dom, window // BS)

    def siblings(piece):
        return [lax.ppermute(piece, "row", [(i, (i + s) % row) for i in range(row)]) for s in range(1, row)]

    def across(piece, shift):
        return lax.ppermute(piece, "wide", [(i, i ^ shift) for i in range(wide)])

    def others(slot, pieces):
        return [(slot, q + 1, piece) for q, piece in enumerate(pieces)]

    shape = jax.ShapeDtypeStruct((2 * window // LANES, row * nq, window, LANES), jnp.bfloat16)
    prepare = functools.partial(screen, read, info)
    mhigh, mlow = mask_amplitudes(read, info, amplitudes)
    if line > 1:
        near, cross = across(factors, 1), across(factors, 2)
        high, low = prepare([(0, 0, factors)], shape)
        cross, high, low, mhigh, mlow = lax.optimization_barrier((cross, high, low, mhigh, mlow))
        last = across(cross, 1)
        early = others(0, siblings(factors)) + [(1, 0, near), (2, 0, cross)]
        s_cross, s_near = siblings(cross), siblings(near)
        high, low = prepare(early, shape, (high, low))
        last, high, low = lax.optimization_barrier((last, high, low))
        late = others(3, siblings(last))
        high, low = prepare([(3, 0, last)] + others(1, s_near) + others(2, s_cross), shape, (high, low))
    else:
        whole = lax.all_gather(factors, "wide", axis=1, tiled=True)
        late = []
        high, low = prepare([(0, 0, whole)] + others(0, siblings(whole)), shape)

    terms = contract_pairs(read, row, col, line, info, late, mhigh, mlow, high, low)
    moved = [lax.ppermute(terms[s], "col", [(i, partner(i, s, col)) for i in range(col)])
             for s in sorted(range(1, col), key=lambda s: -bin(s).count("1"))]
    return add_terms(terms[0], *moved)


def solution(mesh):
    wide, row, col = (mesh.shape[name] for name in ("wide", "row", "col"))
    return jax.shard_map(
        functools.partial(body, wide, row, col),
        mesh=mesh,
        in_specs=(
            P("wide", None, None),
            P(("row", "col"), "wide", None),
            P("wide", None),
            P("wide", None),
            P(),
        ),
        out_specs=P("wide", ("row", "col"), None),
        check_vma=False,
    )
```

```python
import functools

import jax
import jax.numpy as jnp
from jax import lax
from jax.experimental import pallas as pl
from jax.experimental.pallas import tpu as pltpu
from jax.sharding import PartitionSpec as P

BS = 64
LANES = 128
LINE = 4
VMEM_LIMIT = 40 * 1024 * 1024
SMEM_SPEC = pl.BlockSpec(memory_space=pltpu.SMEM)
VMEM_SPEC = pl.BlockSpec(memory_space=pltpu.VMEM)


def split(value):
    top = value.astype(jnp.bfloat16)
    return top, (value - top.astype(jnp.float32)).astype(jnp.bfloat16)


def partner(index, shift, size):
    if size & (size - 1) == 0:
        return index ^ shift
    return (index + shift) % size


def left_of(rows):
    return lax.broadcasted_iota(jnp.int32, (rows, LANES), 1) < BS


class Scalars:
    def __init__(self, info, col, pairs, dom, blocks):
        self.info, self.pairs, self.blocks = info, pairs, blocks
        self.domains = 2 + col
        self.flags = self.domains + dom * pairs
        self.mask = self.flags + dom * pairs

    def place(self, at):
        return self.info[at]

    def domain(self, at, pair):
        return self.info[self.domains + at * self.pairs + pair]

    def flag(self, at, pair):
        return self.info[self.flags + at * self.pairs + pair].astype(jnp.float32)

    def kept(self, first, second):
        return self.info[self.mask + first * self.blocks + second].astype(jnp.float32)


def mask_amplitudes_kernel(read, info, amplitudes, high, low):
    scalars = read(info)
    pairs, domv, _ = amplitudes.shape
    left_half = left_of(1)

    for p in range(pairs):
        for j in range(domv // LANES):
            row = jnp.where(left_half, scalars.flag(2 * j, p), scalars.flag(2 * j + 1, p))
            lanes = slice(j * LANES, (j + 1) * LANES)
            for i in range(domv // BS):
                rows = slice(i * BS, (i + 1) * BS)
                top, rest = split(amplitudes[p, rows, lanes] * (row * scalars.flag(i, p)))
                high[p, rows, lanes] = top
                low[p, rows, lanes] = rest


def mask_amplitudes(read, info, amplitudes):
    shape = jax.ShapeDtypeStruct(amplitudes.shape, jnp.bfloat16)
    return pl.pallas_call(
        functools.partial(mask_amplitudes_kernel, read),
        name="mask_amplitudes",
        out_shape=[shape] * 2,
        in_specs=[SMEM_SPEC, VMEM_SPEC],
        out_specs=[VMEM_SPEC] * 2,
        compiler_params=pltpu.CompilerParams(vmem_limit_bytes=VMEM_LIMIT),
        cost_estimate=pl.CostEstimate(flops=4 * amplitudes.size, bytes_accessed=8 * amplitudes.size, transcendentals=0),
    )(info, amplitudes)


def screen_piece(scalars, piece, q, slot, high, low):
    nq, rows, window = piece.shape
    tiles = window // LANES
    per_slot = rows // BS
    left_half = left_of(1)

    for t in range(tiles):
        lanes = slice(t * LANES, (t + 1) * LANES)
        for h in range(per_slot):
            block = (scalars.place(0) ^ slot) * per_slot + h
            row = jnp.where(left_half, scalars.kept(block, 2 * t), scalars.kept(block, 2 * t + 1))
            target = slice(slot * rows + h * BS, slot * rows + (h + 1) * BS)
            for n in range(nq):
                tile = piece[n, h * BS:(h + 1) * BS, lanes] * row
                for turn, value in ((0, tile), (1, pltpu.roll(tile, BS, 1))):
                    top, rest = split(value)
                    high[turn * tiles + t, q * nq + n, target, :] = top
                    low[turn * tiles + t, q * nq + n, target, :] = rest


def screen_kernel(read, keys, info, *refs):
    high, low = refs[-2:]
    for (slot, q), piece in zip(keys, refs):
        screen_piece(read(info), piece, q, slot, high, low)


def screen(read, info, keyed, shape, held=()):
    keys = [(slot, q) for slot, q, _ in keyed]
    pieces = [piece for _, _, piece in keyed]
    size = sum(piece.size for piece in pieces)
    return pl.pallas_call(
        functools.partial(screen_kernel, read, keys),
        name="screen_factors",
        out_shape=[shape] * 2,
        in_specs=[SMEM_SPEC] + [VMEM_SPEC] * (len(pieces) + len(held)),
        out_specs=[VMEM_SPEC] * 2,
        input_output_aliases={1 + len(pieces) + i: i for i in range(len(held))},
        compiler_params=pltpu.CompilerParams(vmem_limit_bytes=VMEM_LIMIT),
        cost_estimate=pl.CostEstimate(flops=8 * size, bytes_accessed=12 * size, transcendentals=0),
    )(info, *pieces, *held)


def pairs_kernel(read, row, line, late, info, *refs):
    scalars = read(info)
    pieces = refs[:len(late)]
    mhigh, mlow, _, _ = refs[len(late):len(late) + 4]
    outs = refs[len(late) + 4:-2]
    high, low = refs[-2:]
    z, r = scalars.place(0), scalars.place(1)
    for (slot, q), piece in zip(late, pieces):

        @pl.when(z >= 0)
        def _():
            screen_piece(scalars, piece, q, slot, high, low)

    pairs, chunk, domv = outs[0].shape
    twice, qs, window, _ = high.shape
    tiles = twice // 2
    rows = window // line
    per_slot = rows // BS
    half = domv // row
    picks = [r * half + scalars.place(2 + s) * chunk for s in range(len(outs))]
    across = (((1,), (1,)), ((), ()))
    along = (((1,), (0,)), ((), ()))
    dot = functools.partial(lax.dot_general, preferred_element_type=jnp.float32)

    def contract(p):
        def rows_of(at, offset, size):
            block = scalars.domain(at, p)
            start = ((block // per_slot) ^ z) * rows + (block % per_slot) * BS + offset
            return pl.ds(pl.multiple_of(start, size), size)

        sources = []
        for j in range(domv // LANES):
            first, second = scalars.domain(2 * j, p), scalars.domain(2 * j + 1, p)
            sources.append(((first % 2) * tiles + first // 2, (1 - second % 2) * tiles + second // 2))

        def gather(source, q, spans, size):
            return jnp.concatenate([jnp.concatenate([
                jnp.where(left_of(size), source[a, q, span, :], source[b, q, span, :]) for a, b in sources], 1)
                for span in spans], 0)

        spans = [rows_of(i, 0, BS) for i in range(domv // BS)]
        yhigh, ylow = (jnp.concatenate([gather(source, q, spans, BS) for q in range(qs)], 1) for source in (high, low))
        spans = [rows_of(pick // BS, pick % BS, chunk) for pick in picks]
        xhigh, xlow = (jnp.concatenate([gather(source, q, spans, chunk) for q in range(qs)], 0) for source in (high, low))
        both = dot(jnp.concatenate([xhigh, xlow], 0), mhigh[p], along)
        size = qs * half
        halfway = both[:size] + both[size:] + dot(xhigh, mlow[p], along)
        hhigh, hlow = split(jnp.concatenate([halfway[q * half:(q + 1) * half] for q in range(qs)], 1))
        both = dot(jnp.concatenate([hhigh, hlow], 0), yhigh, across)
        total = both[:half] + both[half:] + dot(hhigh, ylow, across)
        for j in range(domv // LANES):
            weights = jnp.where(left_of(1), scalars.flag(2 * j, p), scalars.flag(2 * j + 1, p))
            for n, (pick, out) in enumerate(zip(picks, outs)):
                out[p, :, j * LANES:(j + 1) * LANES] = total[
                    n * chunk:(n + 1) * chunk, j * LANES:(j + 1) * LANES] * (weights * scalars.flag(pick // BS, p))

    for p in range(pairs):
        contract(p)


def contract_pairs(read, row, col, line, info, late, mhigh, mlow, high, low):
    pairs, domv, _ = mhigh.shape
    chunk = domv // (row * col)
    qs = high.shape[1]
    keys = [(slot, q) for slot, q, _ in late]
    pieces = [piece for _, _, piece in late]
    held = 1 + len(pieces) + 2
    results = pl.pallas_call(
        functools.partial(pairs_kernel, read, row, line, keys),
        name="contract_pairs",
        out_shape=[jax.ShapeDtypeStruct((pairs, chunk, domv), jnp.float32)] * col
        + [jax.ShapeDtypeStruct(high.shape, high.dtype)] * 2,
        in_specs=[SMEM_SPEC] + [VMEM_SPEC] * (len(pieces) + 4),
        out_specs=[VMEM_SPEC] * (col + 2),
        input_output_aliases={held: col, held + 1: col + 1},
        compiler_params=pltpu.CompilerParams(vmem_limit_bytes=VMEM_LIMIT),
        cost_estimate=pl.CostEstimate(flops=6 * pairs * qs * domv ** 3 * 4 // row, bytes_accessed=8 * high.size,
                                      transcendentals=0),
    )(info, *pieces, mhigh, mlow, high, low)
    return results[:col]


def add_kernel(*refs):
    total = refs[0][...]
    for ref in refs[1:-1]:
        total += ref[...]
    refs[-1][...] = total


def add_terms(*terms):
    return pl.pallas_call(
        add_kernel,
        name="add_terms",
        out_shape=jax.ShapeDtypeStruct(terms[0].shape, jnp.float32),
        in_specs=[VMEM_SPEC] * len(terms),
        out_specs=VMEM_SPEC,
        compiler_params=pltpu.CompilerParams(vmem_limit_bytes=VMEM_LIMIT),
    )(*terms)


def body(wide, row, col, amplitudes, factors, domains, domain_mask, block_mask):
    nq, rows, window = factors.shape
    pairs, dom = domains.shape
    z, r, c = lax.axis_index("wide"), lax.axis_index("row"), lax.axis_index("col")
    line = wide if wide == LINE and rows % BS == 0 else 1
    place = jnp.stack([z if line > 1 else jnp.zeros_like(z), r] + [partner(c, s, col) for s in range(col)])
    info = jnp.concatenate([place.astype(jnp.int32), domains.T.reshape(-1), domain_mask.T.reshape(-1), block_mask.reshape(-1)])

    def read(ref):
        return Scalars(ref, col, pairs, dom, window // BS)

    def siblings(piece):
        return [lax.ppermute(piece, "row", [(i, (i + s) % row) for i in range(row)]) for s in range(1, row)]

    def across(piece, shift):
        return lax.ppermute(piece, "wide", [(i, i ^ shift) for i in range(wide)])

    def others(slot, pieces):
        return [(slot, q + 1, piece) for q, piece in enumerate(pieces)]

    shape = jax.ShapeDtypeStruct((2 * window // LANES, row * nq, window, LANES), jnp.bfloat16)
    prepare = functools.partial(screen, read, info)
    mhigh, mlow = mask_amplitudes(read, info, amplitudes)
    if line > 1:
        near, cross = across(factors, 1), across(factors, 2)
        high, low = prepare([(0, 0, factors)], shape)
        cross, high, low, mhigh, mlow = lax.optimization_barrier((cross, high, low, mhigh, mlow))
        last = across(cross, 1)
        early = others(0, siblings(factors)) + [(1, 0, near), (2, 0, cross)]
        s_cross, s_near = siblings(cross), siblings(near)
        high, low = prepare(early, shape, (high, low))
        last, high, low = lax.optimization_barrier((last, high, low))
        late = others(3, siblings(last))
        high, low = prepare([(3, 0, last)] + others(1, s_near) + others(2, s_cross), shape, (high, low))
    else:
        whole = lax.all_gather(factors, "wide", axis=1, tiled=True)
        late = []
        high, low = prepare([(0, 0, whole)] + others(0, siblings(whole)), shape)

    terms = contract_pairs(read, row, col, line, info, late, mhigh, mlow, high, low)
    moved = [lax.ppermute(terms[s], "col", [(i, partner(i, s, col)) for i in range(col)])
             for s in sorted(range(1, col), key=lambda s: -bin(s).count("1"))]
    return add_terms(terms[0], *moved)


def solution(mesh):
    wide, row, col = (mesh.shape[name] for name in ("wide", "row", "col"))
    return jax.shard_map(
        functools.partial(body, wide, row, col),
        mesh=mesh,
        in_specs=(
            P("wide", None, None),
            P(("row", "col"), "wide", None),
            P("wide", None),
            P("wide", None),
            P(),
        ),
        out_specs=P("wide", ("row", "col"), None),
        check_vma=False,
    )
```

```python
import functools

import jax
import jax.numpy as jnp
from jax import lax
from jax.experimental import pallas as pl
from jax.experimental.pallas import tpu as pltpu
from jax.sharding import PartitionSpec as P

BS = 64
LANES = 128
LINE = 4
VMEM_LIMIT = 40 * 1024 * 1024
SMEM_SPEC = pl.BlockSpec(memory_space=pltpu.SMEM)
VMEM_SPEC = pl.BlockSpec(memory_space=pltpu.VMEM)


def split(value):
    top = value.astype(jnp.bfloat16)
    return top, (value - top.astype(jnp.float32)).astype(jnp.bfloat16)


def axis_of(r, order):
    return 1 + (r + order) % 2


def left_of(rows):
    return lax.broadcasted_iota(jnp.int32, (rows, LANES), 1) < BS


class Scalars:
    def __init__(self, info, places, pairs, dom, blocks):
        self.info, self.pairs, self.blocks = info, pairs, blocks
        self.domains = places
        self.flags = self.domains + dom * pairs
        self.mask = self.flags + dom * pairs

    def place(self, at):
        return self.info[at]

    def domain(self, at, pair):
        return self.info[self.domains + at * self.pairs + pair]

    def flag(self, at, pair):
        return self.info[self.flags + at * self.pairs + pair].astype(jnp.float32)

    def kept(self, first, second):
        return self.info[self.mask + first * self.blocks + second].astype(jnp.float32)


def mask_amplitudes_kernel(read, info, amplitudes, high, low):
    scalars = read(info)
    pairs, domv, _ = amplitudes.shape
    left_half = left_of(1)

    for p in range(pairs):
        for j in range(domv // LANES):
            row = jnp.where(left_half, scalars.flag(2 * j, p), scalars.flag(2 * j + 1, p))
            lanes = slice(j * LANES, (j + 1) * LANES)
            for i in range(domv // BS):
                rows = slice(i * BS, (i + 1) * BS)
                top, rest = split(amplitudes[p, rows, lanes] * (row * scalars.flag(i, p)))
                high[p, rows, lanes] = top
                low[p, rows, lanes] = rest


def mask_amplitudes(read, info, amplitudes):
    shape = jax.ShapeDtypeStruct(amplitudes.shape, jnp.bfloat16)
    return pl.pallas_call(
        functools.partial(mask_amplitudes_kernel, read),
        name="mask_amplitudes",
        out_shape=[shape] * 2,
        in_specs=[SMEM_SPEC, VMEM_SPEC],
        out_specs=[VMEM_SPEC] * 2,
        compiler_params=pltpu.CompilerParams(vmem_limit_bytes=VMEM_LIMIT),
        cost_estimate=pl.CostEstimate(flops=4 * amplitudes.size, bytes_accessed=8 * amplitudes.size, transcendentals=0),
    )(info, amplitudes)


def screen_piece(scalars, piece, q, slot, high, low):
    nq, rows, window = piece.shape
    tiles = window // LANES
    per_slot = rows // BS
    left_half = left_of(1)

    for t in range(tiles):
        lanes = slice(t * LANES, (t + 1) * LANES)
        for h in range(per_slot):
            block = (scalars.place(0) ^ slot) * per_slot + h
            row = jnp.where(left_half, scalars.kept(block, 2 * t), scalars.kept(block, 2 * t + 1))
            target = slice(slot * rows + h * BS, slot * rows + (h + 1) * BS)
            for n in range(nq):
                tile = piece[n, h * BS:(h + 1) * BS, lanes] * row
                for turn, value in ((0, tile), (1, pltpu.roll(tile, BS, 1))):
                    top, rest = split(value)
                    high[turn * tiles + t, q * nq + n, target, :] = top
                    low[turn * tiles + t, q * nq + n, target, :] = rest


def screen_kernel(read, keys, info, *refs):
    high, low = refs[-2:]
    for (slot, q), piece in zip(keys, refs):
        screen_piece(read(info), piece, q, slot, high, low)


def screen(read, info, keyed, shape, held=()):
    keys = [(slot, q) for slot, q, _ in keyed]
    pieces = [piece for _, _, piece in keyed]
    size = sum(piece.size for piece in pieces)
    return pl.pallas_call(
        functools.partial(screen_kernel, read, keys),
        name="screen_factors",
        out_shape=[shape] * 2,
        in_specs=[SMEM_SPEC] + [VMEM_SPEC] * (len(pieces) + len(held)),
        out_specs=[VMEM_SPEC] * 2,
        input_output_aliases={1 + len(pieces) + i: i for i in range(len(held))},
        compiler_params=pltpu.CompilerParams(vmem_limit_bytes=VMEM_LIMIT),
        cost_estimate=pl.CostEstimate(flops=8 * size, bytes_accessed=12 * size, transcendentals=0),
    )(info, *pieces, *held)


def pairs_kernel(read, row, line, layout, late, info, *refs):
    scalars = read(info)
    pieces = refs[:len(late)]
    mhigh, mlow, _, _ = refs[len(late):len(late) + 4]
    outs = list(refs[len(late) + 4:-2])
    high, low = refs[-2:]
    z, r = scalars.place(0), scalars.place(1)
    for (slot, q), piece in zip(late, pieces):

        @pl.when(z >= 0)
        def _():
            screen_piece(scalars, piece, q, slot, high, low)

    chunk, domv = outs[0].shape[-2:]
    twice, qs, window, _ = high.shape
    tiles = twice // 2
    rows = window // line
    per_slot = rows // BS
    half = domv // row
    across = (((1,), (1,)), ((), ()))
    along = (((1,), (0,)), ((), ()))
    dot = functools.partial(lax.dot_general, preferred_element_type=jnp.float32)

    def contract(p, picks, targets):
        def rows_of(at, offset, size):
            block = scalars.domain(at, p)
            start = ((block // per_slot) ^ z) * rows + (block % per_slot) * BS + offset
            return pl.ds(pl.multiple_of(start, size), size)

        sources = []
        for j in range(domv // LANES):
            first, second = scalars.domain(2 * j, p), scalars.domain(2 * j + 1, p)
            sources.append(((first % 2) * tiles + first // 2, (1 - second % 2) * tiles + second // 2))

        def gather(source, q, spans, size):
            return jnp.concatenate([jnp.concatenate([
                jnp.where(left_of(size), source[a, q, span, :], source[b, q, span, :]) for a, b in sources], 1)
                for span in spans], 0)

        spans = [rows_of(i, 0, BS) for i in range(domv // BS)]
        yhigh, ylow = (jnp.concatenate([gather(source, q, spans, BS) for q in range(qs)], 1) for source in (high, low))
        spans = [rows_of(pick // BS, pick % BS, chunk) for pick in picks]
        xhigh, xlow = (jnp.concatenate([gather(source, q, spans, chunk) for q in range(qs)], 0) for source in (high, low))
        both = dot(jnp.concatenate([xhigh, xlow], 0), mhigh[p], along)
        size = qs * half
        halfway = both[:size] + both[size:] + dot(xhigh, mlow[p], along)
        hhigh, hlow = split(jnp.concatenate([halfway[q * half:(q + 1) * half] for q in range(qs)], 1))
        both = dot(jnp.concatenate([hhigh, hlow], 0), yhigh, across)
        total = both[:half] + both[half:] + dot(hhigh, ylow, across)
        for j in range(domv // LANES):
            lanes = slice(j * LANES, (j + 1) * LANES)
            weights = jnp.where(left_of(1), scalars.flag(2 * j, p), scalars.flag(2 * j + 1, p))
            for n, (pick, (target, at, pair)) in enumerate(zip(picks, targets)):
                target[at, pair, :, lanes] = total[n * chunk:(n + 1) * chunk, lanes] * (weights * scalars.flag(pick // BS, p))

    for first, count, parts in layout:
        refs_of = [outs.pop(0) for _ in parts]
        picks = [r * half + scalars.place(at) * chunk for part in parts for at in part]
        for n in range(count):
            targets = [(ref, i, n) for ref, part in zip(refs_of, parts) for i in range(len(part))]
            contract(scalars.place(first) + n, picks, targets)


def contract_pairs(read, row, line, layout, info, late, mhigh, mlow, high, low):
    domv = mhigh.shape[1]
    chunk = domv // (row * sum(len(part) for part in layout[0][2]))
    keys = [(slot, q) for slot, q, _ in late]
    pieces = [piece for _, _, piece in late]
    held = 1 + len(pieces) + 2
    shapes = [jax.ShapeDtypeStruct((len(part), count, chunk, domv), jnp.float32) for _, count, parts in layout for part in parts]
    outs = len(shapes)
    results = pl.pallas_call(
        functools.partial(pairs_kernel, read, row, line, layout, keys),
        name="contract_pairs",
        out_shape=shapes + [jax.ShapeDtypeStruct(high.shape, high.dtype)] * 2,
        in_specs=[SMEM_SPEC] + [VMEM_SPEC] * (len(pieces) + 4),
        out_specs=[VMEM_SPEC] * (outs + 2),
        input_output_aliases={held: outs, held + 1: outs + 1},
        compiler_params=pltpu.CompilerParams(vmem_limit_bytes=VMEM_LIMIT),
        cost_estimate=pl.CostEstimate(flops=6 * mhigh.shape[0] * high.shape[1] * domv ** 3 * 4 // row,
                                      bytes_accessed=8 * high.size, transcendentals=0),
    )(info, *pieces, mhigh, mlow, high, low)
    return results[:outs]


def add_one_kernel(at, a, b, out):
    out[...] = a[at] + b[at]


def add_one(at, a, b):
    return pl.pallas_call(
        functools.partial(add_one_kernel, at),
        name="add_one",
        out_shape=jax.ShapeDtypeStruct(a.shape[1:], jnp.float32),
        in_specs=[VMEM_SPEC] * 2,
        out_specs=VMEM_SPEC,
        compiler_params=pltpu.CompilerParams(vmem_limit_bytes=VMEM_LIMIT),
    )(a, b)


def join_kernel(*refs):
    out = refs[-1]
    count = refs[0].shape[1]
    r = lax.axis_index("row")
    for order in range(2):
        kept, other, last = refs[3 * order:3 * order + 3]
        out[pl.ds((r + order) % 2 * count, count)] = kept[0] + other[0] + last[...]


def halve(row, col, terms):
    def along(order):
        return [(i * col + k, i * col + (k ^ axis_of(i, order))) for i in range(row) for k in range(col)]

    (sent_a, kept_a, sent_b, kept_b) = terms
    moved_a = lax.ppermute(sent_a, ("row", "col"), along(0))
    moved_b = lax.ppermute(sent_b, ("row", "col"), along(1))
    last_a = lax.ppermute(add_one(1, kept_a, moved_a), ("row", "col"), along(1))
    last_b = lax.ppermute(add_one(1, kept_b, moved_b), ("row", "col"), along(0))
    count = kept_a.shape[1]
    return pl.pallas_call(
        join_kernel,
        name="join_groups",
        out_shape=jax.ShapeDtypeStruct((2 * count,) + kept_a.shape[2:], jnp.float32),
        in_specs=[VMEM_SPEC] * 6,
        out_specs=VMEM_SPEC,
        compiler_params=pltpu.CompilerParams(vmem_limit_bytes=VMEM_LIMIT),
    )(kept_a, moved_a, last_a, kept_b, moved_b, last_b)


def body(wide, row, col, amplitudes, factors, domains, domain_mask, block_mask):
    nq, rows, window = factors.shape
    pairs, dom = domains.shape
    z, r, c = lax.axis_index("wide"), lax.axis_index("row"), lax.axis_index("col")
    line = wide if wide == LINE and rows % BS == 0 else 1
    halving = col == 4 and pairs % 2 == 0
    place = [z if line > 1 else 0, r]
    layout = []
    if halving:
        for order in range(2):
            axis = axis_of(r, order)
            at = len(place)
            place += [(r + order) % 2 * (pairs // 2), c ^ axis, c ^ 3, c, c ^ axis ^ 3]
            layout.append((at, pairs // 2, ((at + 1, at + 2), (at + 3, at + 4))))
    else:
        place += [0] + list(range(col))
        layout.append((2, pairs, (tuple(range(3, 3 + col)),)))
    place = jnp.stack([jnp.asarray(value, jnp.int32) for value in place])
    info = jnp.concatenate([place, domains.T.reshape(-1), domain_mask.T.reshape(-1), block_mask.reshape(-1)])

    def read(ref):
        return Scalars(ref, place.size, pairs, dom, window // BS)

    def siblings(piece):
        return [lax.ppermute(piece, "row", [(i, (i + s) % row) for i in range(row)]) for s in range(1, row)]

    def across(piece, shift):
        return lax.ppermute(piece, "wide", [(i, i ^ shift) for i in range(wide)])

    def others(slot, pieces):
        return [(slot, q + 1, piece) for q, piece in enumerate(pieces)]

    shape = jax.ShapeDtypeStruct((2 * window // LANES, row * nq, window, LANES), jnp.bfloat16)
    prepare = functools.partial(screen, read, info)
    mhigh, mlow = mask_amplitudes(read, info, amplitudes)
    if line > 1:
        near, cross = across(factors, 1), across(factors, 2)
        high, low = prepare([(0, 0, factors)], shape)
        cross, high, low, mhigh, mlow = lax.optimization_barrier((cross, high, low, mhigh, mlow))
        last = across(cross, 1)
        early = others(0, siblings(factors)) + [(1, 0, near), (2, 0, cross)]
        s_cross, s_near = siblings(cross), siblings(near)
        high, low = prepare(early, shape, (high, low))
        last, high, low = lax.optimization_barrier((last, high, low))
        late = others(3, siblings(last))
        high, low = prepare([(3, 0, last)] + others(1, s_near) + others(2, s_cross), shape, (high, low))
    else:
        whole = lax.all_gather(factors, "wide", axis=1, tiled=True)
        late = []
        high, low = prepare([(0, 0, whole)] + others(0, siblings(whole)), shape)

    terms = contract_pairs(read, row, line, layout, info, late, mhigh, mlow, high, low)
    if halving:
        return halve(row, col, terms)
    return jnp.sum(lax.all_to_all(terms[0], "col", 0, 0, tiled=True), axis=0)


def solution(mesh):
    wide, row, col = (mesh.shape[name] for name in ("wide", "row", "col"))
    return jax.shard_map(
        functools.partial(body, wide, row, col),
        mesh=mesh,
        in_specs=(
            P("wide", None, None),
            P(("row", "col"), "wide", None),
            P("wide", None),
            P("wide", None),
            P(),
        ),
        out_specs=P("wide", ("row", "col"), None),
        check_vma=False,
    )
```

```python
import functools

import jax
import jax.numpy as jnp
from jax import lax
from jax.experimental import pallas as pl
from jax.experimental.pallas import tpu as pltpu
from jax.sharding import PartitionSpec as P

BS = 64
LANES = 128
LINE = 4
VMEM_LIMIT = 40 * 1024 * 1024
VMEM_SPEC = pl.BlockSpec(memory_space=pltpu.VMEM)


def split(value):
    top = value.astype(jnp.bfloat16)
    return top, (value - top.astype(jnp.float32)).astype(jnp.bfloat16)


def partner(index, shift, size):
    if size & (size - 1) == 0:
        return index ^ shift
    return (index + shift) % size


def left_of(rows):
    return lax.broadcasted_iota(jnp.int32, (rows, LANES), 1) < BS


def mask_amplitudes_kernel(weights, amplitudes, high, low):
    pairs, domv, _ = amplitudes.shape
    for p in range(pairs):
        for i in range(domv // BS):
            rows = slice(i * BS, (i + 1) * BS)
            top, rest = split(amplitudes[p, rows, :] * weights[p, i])
            high[p, rows, :] = top
            low[p, rows, :] = rest


def mask_amplitudes(weights, amplitudes):
    shape = jax.ShapeDtypeStruct(amplitudes.shape, jnp.bfloat16)
    return pl.pallas_call(
        mask_amplitudes_kernel,
        name="mask_amplitudes",
        out_shape=[shape] * 2,
        in_specs=[VMEM_SPEC] * 2,
        out_specs=[VMEM_SPEC] * 2,
        compiler_params=pltpu.CompilerParams(vmem_limit_bytes=VMEM_LIMIT),
        cost_estimate=pl.CostEstimate(flops=4 * amplitudes.size, bytes_accessed=8 * amplitudes.size, transcendentals=0),
    )(weights, amplitudes)


def screen_piece(mask, piece, q, slot, high, low):
    nq, rows, window = piece.shape
    tiles = window // LANES
    for h in range(rows // BS):
        block = slot * (rows // BS) + h
        target = slice(block * BS, (block + 1) * BS)
        for t in range(tiles):
            lanes = slice(t * LANES, (t + 1) * LANES)
            for n in range(nq):
                tile = piece[n, h * BS:(h + 1) * BS, lanes] * mask[block, :, lanes]
                for turn, value in ((0, tile), (1, pltpu.roll(tile, BS, 1))):
                    top, rest = split(value)
                    high[turn * tiles + t, q * nq + n, target, :] = top
                    low[turn * tiles + t, q * nq + n, target, :] = rest


def screen_kernel(keys, mask, *refs):
    high, low = refs[-2:]
    for (slot, q), piece in zip(keys, refs):
        screen_piece(mask, piece, q, slot, high, low)


def screen(mask, keyed, shape, held=()):
    keys = [(slot, q) for slot, q, _ in keyed]
    pieces = [piece for _, _, piece in keyed]
    size = sum(piece.size for piece in pieces)
    return pl.pallas_call(
        functools.partial(screen_kernel, keys),
        name="screen_factors",
        out_shape=[shape] * 2,
        in_specs=[VMEM_SPEC] * (1 + len(pieces) + len(held)),
        out_specs=[VMEM_SPEC] * 2,
        input_output_aliases={1 + len(pieces) + i: i for i in range(len(held))},
        compiler_params=pltpu.CompilerParams(vmem_limit_bytes=VMEM_LIMIT),
        cost_estimate=pl.CostEstimate(flops=8 * size, bytes_accessed=12 * size, transcendentals=0),
    )(mask, *pieces, *held)


def pairs_kernel(row, factors, late, last, count, places, mask, weights, *refs):
    pieces = refs[:len(late)]
    mhigh, mlow = refs[len(late):len(late) + 2]
    held = refs[len(late) + 4:-count - 2]
    outs, (high, low) = refs[-count - 2:-2], refs[-2:]
    at = places[...]
    for (slot, q), piece in zip(late, pieces):

        @pl.when(at[0, 0] >= 0)
        def _():
            screen_piece(mask, piece, q, slot, high, low)

    pairs, chunk, domv = outs[0].shape
    qs = len(factors)
    half = domv // row
    blocks = domv // BS
    tiles = domv // LANES
    across = (((1,), (1,)), ((), ()))
    along = (((1,), (0,)), ((), ()))
    dot = functools.partial(lax.dot_general, preferred_element_type=jnp.float32)

    def contract(p):
        def rows_at(n, size):
            return pl.ds(pl.multiple_of(at[0, n * pairs + p], size), size)

        y_spans = [rows_at(i, BS) for i in range(blocks)]
        x_spans = [rows_at(blocks + n, chunk) for n in range(count)]
        first = blocks + count
        sources = [(at[0, (first + 2 * j) * pairs + p], at[0, (first + 2 * j + 1) * pairs + p]) for j in range(tiles)]

        def gather(source, q, spans, size):
            return jnp.concatenate([jnp.concatenate([
                jnp.where(left_of(size), source[a, q, span, :], source[b, q, span, :]) for a, b in sources], 1)
                for span in spans], 0)

        yhigh, ylow = (jnp.concatenate([gather(source, q, y_spans, BS) for q in factors], 1) for source in (high, low))
        xhigh, xlow = (jnp.concatenate([gather(source, q, x_spans, chunk) for q in factors], 0) for source in (high, low))
        both = dot(jnp.concatenate([xhigh, xlow], 0), mhigh[p], along)
        size = qs * half
        halfway = both[:size] + both[size:] + dot(xhigh, mlow[p], along)
        hhigh, hlow = split(jnp.concatenate([halfway[q * half:(q + 1) * half] for q in range(qs)], 1))
        both = dot(jnp.concatenate([hhigh, hlow], 0), yhigh, across)
        total = both[:half] + both[half:] + dot(hhigh, ylow, across)
        for n, out in enumerate(outs):
            term = total[n * chunk:(n + 1) * chunk]
            if held:
                term += held[n][p]
            out[p] = term * weights[n, p] if last else term

    for p in range(pairs):
        contract(p)


def contract_pairs(row, col, places, mask, weights, factors, last, late, mhigh, mlow, high, low, held=()):
    pairs, domv, _ = mhigh.shape
    chunk = domv // (row * col)
    keys = [(slot, q) for slot, q, _ in late]
    pieces = [piece for _, _, piece in late]
    prepared = 3 + len(pieces) + 2
    results = pl.pallas_call(
        functools.partial(pairs_kernel, row, factors, keys, last, col),
        name="contract_pairs",
        out_shape=[jax.ShapeDtypeStruct((pairs, chunk, domv), jnp.float32)] * col
        + [jax.ShapeDtypeStruct(high.shape, high.dtype)] * 2,
        in_specs=[VMEM_SPEC] * (3 + len(pieces) + 4 + len(held)),
        out_specs=[VMEM_SPEC] * (col + 2),
        input_output_aliases={prepared: col, prepared + 1: col + 1},
        compiler_params=pltpu.CompilerParams(vmem_limit_bytes=VMEM_LIMIT),
        cost_estimate=pl.CostEstimate(flops=6 * pairs * len(factors) * domv ** 3 * 4 // row, bytes_accessed=8 * high.size,
                                      transcendentals=0),
    )(places, mask, weights, *pieces, mhigh, mlow, high, low, *held)
    return results[:col], results[col], results[col + 1]


def add_kernel(*refs):
    total = refs[0][...]
    for ref in refs[1:-1]:
        total += ref[...]
    refs[-1][...] = total


def add_terms(*terms):
    return pl.pallas_call(
        add_kernel,
        name="add_terms",
        out_shape=jax.ShapeDtypeStruct(terms[0].shape, jnp.float32),
        in_specs=[VMEM_SPEC] * len(terms),
        out_specs=VMEM_SPEC,
        compiler_params=pltpu.CompilerParams(vmem_limit_bytes=VMEM_LIMIT),
    )(*terms)


def body(wide, row, col, amplitudes, factors, domains, domain_mask, block_mask):
    nq, rows, window = factors.shape
    pairs, dom = domains.shape
    z, r, c = lax.axis_index("wide"), lax.axis_index("row"), lax.axis_index("col")
    line = wide if wide == LINE and rows % BS == 0 else 1
    plane = z if line > 1 else 0
    blocks = window // BS
    per_slot = blocks // line
    domv = dom * BS
    tiles = window // LANES
    half = domv // row
    chunk = half // col

    def pick(which, table):
        hits = which[:, None] == jnp.arange(table.shape[0])[None, :]
        return jnp.sum(jnp.where(hits[:, :, None], table[None], 0), axis=1)

    blocks_of, flags = domains.T, domain_mask.T
    starts = ((blocks_of // per_slot) ^ plane) * (per_slot * BS) + blocks_of % per_slot * BS
    offsets = r * half + jnp.stack([partner(c, s, col) for s in range(col)]) * chunk
    chosen = pick(offsets // BS, starts) + (offsets % BS)[:, None]
    firsts, seconds = blocks_of[0::2], blocks_of[1::2]
    sources = jnp.stack([firsts % 2 * tiles + firsts // 2, (1 - seconds % 2) * tiles + seconds // 2], 1)
    places = jnp.concatenate([starts, chosen, sources.reshape(-1, pairs)], 0).reshape(1, -1)

    order = jnp.arange(blocks)
    kept = pick(((order // per_slot) ^ plane) * per_slot + order % per_slot, block_mask)
    mask = jnp.repeat(kept, BS, axis=1).astype(jnp.float32)[:, None, :]
    lanes = jnp.repeat(domain_mask, BS, axis=1)
    inner = (domain_mask[:, :, None] * lanes[:, None, :]).astype(jnp.float32)[:, :, None, :]
    outer = (pick(offsets // BS, flags)[:, :, None] * lanes[None]).astype(jnp.float32)[:, :, None, :]

    def siblings(piece):
        return [lax.ppermute(piece, "row", [(i, (i + s) % row) for i in range(row)]) for s in range(1, row)]

    def across(piece, shift):
        return lax.ppermute(piece, "wide", [(i, i ^ shift) for i in range(wide)])

    def others(slot, pieces):
        return [(slot, q + 1, piece) for q, piece in enumerate(pieces)]

    shape = jax.ShapeDtypeStruct((2 * window // LANES, row * nq, window, LANES), jnp.bfloat16)
    prepare = functools.partial(screen, mask)
    mhigh, mlow = mask_amplitudes(inner, amplitudes)
    if line > 1:
        near, cross = across(factors, 1), across(factors, 2)
        high, low = prepare([(0, 0, factors)], shape)
        cross, high, low, mhigh, mlow, places, outer = lax.optimization_barrier(
            (cross, high, low, mhigh, mlow, places, outer))
        last = across(cross, 1)
        early = others(0, siblings(factors)) + [(1, 0, near), (2, 0, cross)]
        s_cross, s_near = siblings(cross), siblings(near)
        high, low = prepare(early, shape, (high, low))
        last, high, low = lax.optimization_barrier((last, high, low))
        contract = functools.partial(contract_pairs, row, col, places, mask, outer)
        sent = others(3, siblings(last)) + others(1, s_near) + others(2, s_cross)
        held, high, low = contract(range(nq), False, [(3, 0, last)], mhigh, mlow, high, low)
        terms, _, _ = contract(range(nq, row * nq), True, sent, mhigh, mlow, high, low, held)
    else:
        whole = lax.all_gather(factors, "wide", axis=1, tiled=True)
        high, low = prepare([(0, 0, whole)] + others(0, siblings(whole)), shape)
        contract = functools.partial(contract_pairs, row, col, places, mask, outer)
        terms, _, _ = contract(range(row * nq), True, [], mhigh, mlow, high, low)

    moved = [lax.ppermute(terms[s], "col", [(i, partner(i, s, col)) for i in range(col)])
             for s in sorted(range(1, col), key=lambda s: -bin(s).count("1"))]
    return add_terms(terms[0], *moved)


def solution(mesh):
    wide, row, col = (mesh.shape[name] for name in ("wide", "row", "col"))
    return jax.shard_map(
        functools.partial(body, wide, row, col),
        mesh=mesh,
        in_specs=(
            P("wide", None, None),
            P(("row", "col"), "wide", None),
            P("wide", None),
            P("wide", None),
            P(),
        ),
        out_specs=P("wide", ("row", "col"), None),
        check_vma=False,
    )
```

```python
import functools

import jax
import jax.numpy as jnp
from jax import lax
from jax.experimental import pallas as pl
from jax.experimental.pallas import tpu as pltpu
from jax.sharding import PartitionSpec as P

BS = 64
LANES = 128
LINE = 4
VMEM_LIMIT = 40 * 1024 * 1024
VMEM_SPEC = pl.BlockSpec(memory_space=pltpu.VMEM)


def split(value):
    top = value.astype(jnp.bfloat16)
    return top, (value - top.astype(jnp.float32)).astype(jnp.bfloat16)


def partner(index, shift, size):
    if size & (size - 1) == 0:
        return index ^ shift
    return (index + shift) % size


def left_of(rows):
    return lax.broadcasted_iota(jnp.int32, (rows, LANES), 1) < BS


def mask_amplitudes_kernel(weights, amplitudes, high, low):
    pairs, domv, _ = amplitudes.shape
    for p in range(pairs):
        for i in range(domv // BS):
            rows = slice(i * BS, (i + 1) * BS)
            top, rest = split(amplitudes[p, rows, :] * weights[p, i])
            high[p, rows, :] = top
            low[p, rows, :] = rest


def mask_amplitudes(weights, amplitudes):
    shape = jax.ShapeDtypeStruct(amplitudes.shape, jnp.bfloat16)
    return pl.pallas_call(
        mask_amplitudes_kernel,
        name="mask_amplitudes",
        out_shape=[shape] * 2,
        in_specs=[VMEM_SPEC] * 2,
        out_specs=[VMEM_SPEC] * 2,
        compiler_params=pltpu.CompilerParams(vmem_limit_bytes=VMEM_LIMIT),
        cost_estimate=pl.CostEstimate(flops=4 * amplitudes.size, bytes_accessed=8 * amplitudes.size, transcendentals=0),
    )(weights, amplitudes)


def screen_piece(mask, piece, q, slot, high, low):
    nq, rows, window = piece.shape
    tiles = window // LANES
    for h in range(rows // BS):
        block = slot * (rows // BS) + h
        target = slice(block * BS, (block + 1) * BS)
        for t in range(tiles):
            lanes = slice(t * LANES, (t + 1) * LANES)
            for n in range(nq):
                tile = piece[n, h * BS:(h + 1) * BS, lanes] * mask[block, :, lanes]
                for turn, value in ((0, tile), (1, pltpu.roll(tile, BS, 1))):
                    top, rest = split(value)
                    high[turn * tiles + t, q * nq + n, target, :] = top
                    low[turn * tiles + t, q * nq + n, target, :] = rest


def screen_kernel(keys, mask, *refs):
    high, low = refs[-2:]
    for (slot, q), piece in zip(keys, refs):
        screen_piece(mask, piece, q, slot, high, low)


def screen(mask, keyed, shape, held=()):
    keys = [(slot, q) for slot, q, _ in keyed]
    pieces = [piece for _, _, piece in keyed]
    size = sum(piece.size for piece in pieces)
    return pl.pallas_call(
        functools.partial(screen_kernel, keys),
        name="screen_factors",
        out_shape=[shape] * 2,
        in_specs=[VMEM_SPEC] * (1 + len(pieces) + len(held)),
        out_specs=[VMEM_SPEC] * 2,
        input_output_aliases={1 + len(pieces) + i: i for i in range(len(held))},
        compiler_params=pltpu.CompilerParams(vmem_limit_bytes=VMEM_LIMIT),
        cost_estimate=pl.CostEstimate(flops=8 * size, bytes_accessed=12 * size, transcendentals=0),
    )(mask, *pieces, *held)


def pairs_kernel(row, col, factors, late, last, shifts, places, mask, weights, *refs):
    pieces = refs[:len(late)]
    mhigh, mlow = refs[len(late):len(late) + 2]
    count = len(shifts)
    held = refs[len(late) + 4:-count - 2]
    outs, (high, low) = refs[-count - 2:-2], refs[-2:]
    at = places[...]
    for (slot, q), piece in zip(late, pieces):

        @pl.when(at[0, 0] >= 0)
        def _():
            screen_piece(mask, piece, q, slot, high, low)

    pairs, chunk, domv = outs[0].shape
    qs = len(factors)
    size = count * chunk
    blocks = domv // BS
    tiles = domv // LANES
    across = (((1,), (1,)), ((), ()))
    along = (((1,), (0,)), ((), ()))
    dot = functools.partial(lax.dot_general, preferred_element_type=jnp.float32)

    def contract(p):
        def rows_at(n, size):
            return pl.ds(pl.multiple_of(at[0, n * pairs + p], size), size)

        y_spans = [rows_at(i, BS) for i in range(blocks)]
        x_spans = [rows_at(blocks + n, chunk) for n in shifts]
        first = blocks + col
        sources = [(at[0, (first + 2 * j) * pairs + p], at[0, (first + 2 * j + 1) * pairs + p]) for j in range(tiles)]

        def gather(source, q, spans, size):
            return jnp.concatenate([jnp.concatenate([
                jnp.where(left_of(size), source[a, q, span, :], source[b, q, span, :]) for a, b in sources], 1)
                for span in spans], 0)

        yhigh, ylow = (jnp.concatenate([gather(source, q, y_spans, BS) for q in factors], 1) for source in (high, low))
        xhigh, xlow = (jnp.concatenate([gather(source, q, x_spans, chunk) for q in factors], 0) for source in (high, low))
        both = dot(jnp.concatenate([xhigh, xlow], 0), mhigh[p], along)
        halfway = both[:qs * size] + both[qs * size:] + dot(xhigh, mlow[p], along)
        hhigh, hlow = split(jnp.concatenate([halfway[q * size:(q + 1) * size] for q in range(qs)], 1))
        both = dot(jnp.concatenate([hhigh, hlow], 0), yhigh, across)
        total = both[:size] + both[size:] + dot(hhigh, ylow, across)
        for n, (shift, out) in enumerate(zip(shifts, outs)):
            term = total[n * chunk:(n + 1) * chunk]
            if held:
                term += held[shift][p]
            out[p] = term * weights[shift, p] if last else term

    for p in range(pairs):
        contract(p)


def contract_pairs(row, col, places, mask, weights, factors, last, shifts, late, mhigh, mlow, high, low, held=()):
    pairs, domv, _ = mhigh.shape
    chunk = domv // (row * col)
    keys = [(slot, q) for slot, q, _ in late]
    pieces = [piece for _, _, piece in late]
    prepared = 3 + len(pieces) + 2
    count = len(shifts)
    results = pl.pallas_call(
        functools.partial(pairs_kernel, row, col, factors, keys, last, shifts),
        name="contract_pairs",
        out_shape=[jax.ShapeDtypeStruct((pairs, chunk, domv), jnp.float32)] * count
        + [jax.ShapeDtypeStruct(high.shape, high.dtype)] * 2,
        in_specs=[VMEM_SPEC] * (3 + len(pieces) + 4 + len(held)),
        out_specs=[VMEM_SPEC] * (count + 2),
        input_output_aliases={prepared: count, prepared + 1: count + 1},
        compiler_params=pltpu.CompilerParams(vmem_limit_bytes=VMEM_LIMIT),
        cost_estimate=pl.CostEstimate(flops=6 * pairs * len(factors) * domv ** 3 * 4 * count // (row * col), bytes_accessed=8 * high.size,
                                      transcendentals=0),
    )(places, mask, weights, *pieces, mhigh, mlow, high, low, *held)
    return results[:count], results[count], results[count + 1]


def add_kernel(*refs):
    total = refs[0][...]
    for ref in refs[1:-1]:
        total += ref[...]
    refs[-1][...] = total


def add_terms(*terms, ahead=0):
    return pl.pallas_call(
        add_kernel,
        name="add_terms",
        out_shape=jax.ShapeDtypeStruct(terms[0].shape, jnp.float32),
        in_specs=[VMEM_SPEC] * len(terms),
        out_specs=VMEM_SPEC,
        compiler_params=pltpu.CompilerParams(vmem_limit_bytes=VMEM_LIMIT),
        cost_estimate=pl.CostEstimate(flops=0, bytes_accessed=ahead + 4 * len(terms) * terms[0].size, transcendentals=0),
    )(*terms)


def body(wide, row, col, amplitudes, factors, domains, domain_mask, block_mask):
    nq, rows, window = factors.shape
    pairs, dom = domains.shape
    z, r, c = lax.axis_index("wide"), lax.axis_index("row"), lax.axis_index("col")
    line = wide if wide == LINE and rows % BS == 0 else 1
    plane = z if line > 1 else 0
    blocks = window // BS
    per_slot = blocks // line
    domv = dom * BS
    tiles = window // LANES
    half = domv // row
    chunk = half // col

    def pick(which, table):
        hits = which[:, None] == jnp.arange(table.shape[0])[None, :]
        return jnp.sum(jnp.where(hits[:, :, None], table[None], 0), axis=1)

    shifts = sorted(range(col), key=lambda s: -bin(s).count("1"))

    blocks_of, flags = domains.T, domain_mask.T
    starts = ((blocks_of // per_slot) ^ plane) * (per_slot * BS) + blocks_of % per_slot * BS
    offsets = r * half + jnp.stack([partner(c, s, col) for s in range(col)]) * chunk
    chosen = pick(offsets // BS, starts) + (offsets % BS)[:, None]
    firsts, seconds = blocks_of[0::2], blocks_of[1::2]
    sources = jnp.stack([firsts % 2 * tiles + firsts // 2, (1 - seconds % 2) * tiles + seconds // 2], 1)
    places = jnp.concatenate([starts, chosen, sources.reshape(-1, pairs)], 0).reshape(1, -1)

    order = jnp.arange(blocks)
    kept = pick(((order // per_slot) ^ plane) * per_slot + order % per_slot, block_mask)
    mask = jnp.repeat(kept, BS, axis=1).astype(jnp.float32)[:, None, :]
    lanes = jnp.repeat(domain_mask, BS, axis=1)
    inner = (domain_mask[:, :, None] * lanes[:, None, :]).astype(jnp.float32)[:, :, None, :]
    outer = (pick(offsets // BS, flags)[:, :, None] * lanes[None]).astype(jnp.float32)[:, :, None, :]

    def siblings(piece):
        return [lax.ppermute(piece, "row", [(i, (i + s) % row) for i in range(row)]) for s in range(1, row)]

    def across(piece, shift):
        return lax.ppermute(piece, "wide", [(i, i ^ shift) for i in range(wide)])

    def others(slot, pieces):
        return [(slot, q + 1, piece) for q, piece in enumerate(pieces)]

    shape = jax.ShapeDtypeStruct((2 * window // LANES, row * nq, window, LANES), jnp.bfloat16)
    prepare = functools.partial(screen, mask)
    mhigh, mlow = mask_amplitudes(inner, amplitudes)
    if line > 1:
        near, cross = across(factors, 1), across(factors, 2)
        high, low = prepare([(0, 0, factors)], shape)
        cross, high, low, mhigh, mlow, places, outer = lax.optimization_barrier(
            (cross, high, low, mhigh, mlow, places, outer))
        last = across(cross, 1)
        early = others(0, siblings(factors)) + [(1, 0, near), (2, 0, cross)]
        s_cross, s_near = siblings(cross), siblings(near)
        high, low = prepare(early, shape, (high, low))
        last, high, low = lax.optimization_barrier((last, high, low))
        contract = functools.partial(contract_pairs, row, col, places, mask, outer)
        sent = others(3, siblings(last)) + others(1, s_near) + others(2, s_cross)
        held, high, low = contract(range(nq), False, range(col), [(3, 0, last)], mhigh, mlow, high, low)
        far, high, low = contract(range(nq, row * nq), True, shifts[:1], sent, mhigh, mlow, high, low, held)
        rest, _, _ = contract(range(nq, row * nq), True, shifts[1:], [], mhigh, mlow, high, low, held)
        terms = dict(zip(shifts, far + rest))
    else:
        whole = lax.all_gather(factors, "wide", axis=1, tiled=True)
        high, low = prepare([(0, 0, whole)] + others(0, siblings(whole)), shape)
        contract = functools.partial(contract_pairs, row, col, places, mask, outer)
        rest, _, _ = contract(range(row * nq), True, shifts, [], mhigh, mlow, high, low)
        terms = dict(zip(shifts, rest))

    moved = [lax.ppermute(terms[s], "col", [(i, partner(i, s, col)) for i in range(col)]) for s in shifts if s]
    return add_terms(add_terms(terms[0], moved[0], ahead=1 << 24), *moved[1:])


def solution(mesh):
    wide, row, col = (mesh.shape[name] for name in ("wide", "row", "col"))
    return jax.shard_map(
        functools.partial(body, wide, row, col),
        mesh=mesh,
        in_specs=(
            P("wide", None, None),
            P(("row", "col"), "wide", None),
            P("wide", None),
            P("wide", None),
            P(),
        ),
        out_specs=P("wide", ("row", "col"), None),
        check_vma=False,
    )
```

```python
import functools

import jax
import jax.numpy as jnp
from jax import lax
from jax.experimental import pallas as pl
from jax.experimental.pallas import tpu as pltpu
from jax.sharding import PartitionSpec as P

BS = 64
LANES = 128
LINE = 4
VMEM_LIMIT = 40 * 1024 * 1024
VMEM_SPEC = pl.BlockSpec(memory_space=pltpu.VMEM)


def split(value):
    top = value.astype(jnp.bfloat16)
    return top, (value - top.astype(jnp.float32)).astype(jnp.bfloat16)


def partner(index, shift, size):
    if size & (size - 1) == 0:
        return index ^ shift
    return (index + shift) % size


def left_of(rows):
    return lax.broadcasted_iota(jnp.int32, (rows, LANES), 1) < BS


def mask_amplitudes_kernel(weights, amplitudes, high, low):
    pairs, domv, _ = amplitudes.shape
    for p in range(pairs):
        for i in range(domv // BS):
            rows = slice(i * BS, (i + 1) * BS)
            top, rest = split(amplitudes[p, rows, :] * weights[p, i])
            high[p, rows, :] = top
            low[p, rows, :] = rest


def mask_amplitudes(weights, amplitudes):
    shape = jax.ShapeDtypeStruct(amplitudes.shape, jnp.bfloat16)
    return pl.pallas_call(
        mask_amplitudes_kernel,
        name="mask_amplitudes",
        out_shape=[shape] * 2,
        in_specs=[VMEM_SPEC] * 2,
        out_specs=[VMEM_SPEC] * 2,
        compiler_params=pltpu.CompilerParams(vmem_limit_bytes=VMEM_LIMIT),
        cost_estimate=pl.CostEstimate(flops=4 * amplitudes.size, bytes_accessed=8 * amplitudes.size, transcendentals=0),
    )(weights, amplitudes)


def screen_piece(mask, piece, q, slot, high, low):
    nq, rows, window = piece.shape
    tiles = window // LANES
    for h in range(rows // BS):
        block = slot * (rows // BS) + h
        target = slice(block * BS, (block + 1) * BS)
        for t in range(tiles):
            lanes = slice(t * LANES, (t + 1) * LANES)
            for n in range(nq):
                tile = piece[n, h * BS:(h + 1) * BS, lanes] * mask[block, :, lanes]
                for turn, value in ((0, tile), (1, pltpu.roll(tile, BS, 1))):
                    top, rest = split(value)
                    high[turn * tiles + t, q * nq + n, target, :] = top
                    low[turn * tiles + t, q * nq + n, target, :] = rest


def screen_kernel(keys, mask, *refs):
    high, low = refs[-2:]
    for (slot, q), piece in zip(keys, refs):
        screen_piece(mask, piece, q, slot, high, low)


def screen(mask, keyed, shape, held=()):
    keys = [(slot, q) for slot, q, _ in keyed]
    pieces = [piece for _, _, piece in keyed]
    size = sum(piece.size for piece in pieces)
    return pl.pallas_call(
        functools.partial(screen_kernel, keys),
        name="screen_factors",
        out_shape=[shape] * 2,
        in_specs=[VMEM_SPEC] * (1 + len(pieces) + len(held)),
        out_specs=[VMEM_SPEC] * 2,
        input_output_aliases={1 + len(pieces) + i: i for i in range(len(held))},
        compiler_params=pltpu.CompilerParams(vmem_limit_bytes=VMEM_LIMIT),
        cost_estimate=pl.CostEstimate(flops=8 * size, bytes_accessed=12 * size, transcendentals=0),
    )(mask, *pieces, *held)


def pairs_kernel(row, col, factors, late, last, shifts, places, mask, weights, *refs):
    pieces = refs[:len(late)]
    mhigh, mlow = refs[len(late):len(late) + 2]
    count = len(shifts)
    held = refs[len(late) + 4:-count - 2]
    outs, (high, low) = refs[-count - 2:-2], refs[-2:]
    at = places[...]
    for (slot, q), piece in zip(late, pieces):

        @pl.when(at[0, 0] >= 0)
        def _():
            screen_piece(mask, piece, q, slot, high, low)

    pairs, chunk, domv = outs[0].shape
    qs = len(factors)
    size = count * chunk
    blocks = domv // BS
    tiles = domv // LANES
    across = (((1,), (1,)), ((), ()))
    along = (((1,), (0,)), ((), ()))
    dot = functools.partial(lax.dot_general, preferred_element_type=jnp.float32)

    def contract(p):
        def rows_at(n, size):
            return pl.ds(pl.multiple_of(at[0, n * pairs + p], size), size)

        y_spans = [rows_at(i, BS) for i in range(blocks)]
        x_spans = [rows_at(blocks + n, chunk) for n in shifts]
        first = blocks + col
        sources = [(at[0, (first + 2 * j) * pairs + p], at[0, (first + 2 * j + 1) * pairs + p]) for j in range(tiles)]

        def gather(source, q, spans, size):
            return jnp.concatenate([jnp.concatenate([
                jnp.where(left_of(size), source[a, q, span, :], source[b, q, span, :]) for a, b in sources], 1)
                for span in spans], 0)

        yhigh, ylow = (jnp.concatenate([gather(source, q, y_spans, BS) for q in factors], 1) for source in (high, low))
        xhigh, xlow = (jnp.concatenate([gather(source, q, x_spans, chunk) for q in factors], 0) for source in (high, low))
        both = dot(jnp.concatenate([xhigh, xlow], 0), mhigh[p], along)
        halfway = both[:qs * size] + both[qs * size:] + dot(xhigh, mlow[p], along)
        hhigh, hlow = split(jnp.concatenate([halfway[q * size:(q + 1) * size] for q in range(qs)], 1))
        both = dot(jnp.concatenate([hhigh, hlow], 0), yhigh, across)
        total = both[:size] + both[size:] + dot(hhigh, ylow, across)
        for n, (shift, out) in enumerate(zip(shifts, outs)):
            term = total[n * chunk:(n + 1) * chunk]
            if held:
                term += held[n][p]
            out[p] = term * weights[shift, p] if last else term

    for p in range(pairs):
        contract(p)


def contract_pairs(row, col, places, mask, weights, factors, last, shifts, late, mhigh, mlow, high, low, held=()):
    pairs, domv, _ = mhigh.shape
    chunk = domv // (row * col)
    keys = [(slot, q) for slot, q, _ in late]
    pieces = [piece for _, _, piece in late]
    prepared = 3 + len(pieces) + 2
    count = len(shifts)
    results = pl.pallas_call(
        functools.partial(pairs_kernel, row, col, factors, keys, last, shifts),
        name="contract_pairs",
        out_shape=[jax.ShapeDtypeStruct((pairs, chunk, domv), jnp.float32)] * count
        + [jax.ShapeDtypeStruct(high.shape, high.dtype)] * 2,
        in_specs=[VMEM_SPEC] * (3 + len(pieces) + 4 + len(held)),
        out_specs=[VMEM_SPEC] * (count + 2),
        input_output_aliases={prepared: count, prepared + 1: count + 1},
        compiler_params=pltpu.CompilerParams(vmem_limit_bytes=VMEM_LIMIT),
        cost_estimate=pl.CostEstimate(flops=6 * pairs * len(factors) * domv ** 3 * 4 * count // (row * col), bytes_accessed=8 * high.size,
                                      transcendentals=0),
    )(places, mask, weights, *pieces, mhigh, mlow, high, low, *held)
    return results[:count], results[count], results[count + 1]


def add_kernel(*refs):
    total = refs[0][...]
    for ref in refs[1:-1]:
        total += ref[...]
    refs[-1][...] = total


def add_terms(*terms, ahead=0):
    return pl.pallas_call(
        add_kernel,
        name="add_terms",
        out_shape=jax.ShapeDtypeStruct(terms[0].shape, jnp.float32),
        in_specs=[VMEM_SPEC] * len(terms),
        out_specs=VMEM_SPEC,
        compiler_params=pltpu.CompilerParams(vmem_limit_bytes=VMEM_LIMIT),
        cost_estimate=pl.CostEstimate(flops=0, bytes_accessed=ahead + 4 * len(terms) * terms[0].size, transcendentals=0),
    )(*terms)


def body(wide, row, col, amplitudes, factors, domains, domain_mask, block_mask):
    nq, rows, window = factors.shape
    pairs, dom = domains.shape
    z, r, c = lax.axis_index("wide"), lax.axis_index("row"), lax.axis_index("col")
    line = wide if wide == LINE and rows % BS == 0 else 1
    plane = z if line > 1 else 0
    blocks = window // BS
    per_slot = blocks // line
    domv = dom * BS
    tiles = window // LANES
    half = domv // row
    chunk = half // col

    def pick(which, table):
        hits = which[:, None] == jnp.arange(table.shape[0])[None, :]
        return jnp.sum(jnp.where(hits[:, :, None], table[None], 0), axis=1)

    shifts = sorted(range(col), key=lambda s: -bin(s).count("1"))

    blocks_of, flags = domains.T, domain_mask.T
    starts = ((blocks_of // per_slot) ^ plane) * (per_slot * BS) + blocks_of % per_slot * BS
    offsets = r * half + jnp.stack([partner(c, s, col) for s in range(col)]) * chunk
    chosen = pick(offsets // BS, starts) + (offsets % BS)[:, None]
    firsts, seconds = blocks_of[0::2], blocks_of[1::2]
    sources = jnp.stack([firsts % 2 * tiles + firsts // 2, (1 - seconds % 2) * tiles + seconds // 2], 1)
    places = jnp.concatenate([starts, chosen, sources.reshape(-1, pairs)], 0).reshape(1, -1)

    order = jnp.arange(blocks)
    kept = pick(((order // per_slot) ^ plane) * per_slot + order % per_slot, block_mask)
    mask = jnp.repeat(kept, BS, axis=1).astype(jnp.float32)[:, None, :]
    lanes = jnp.repeat(domain_mask, BS, axis=1)
    inner = (domain_mask[:, :, None] * lanes[:, None, :]).astype(jnp.float32)[:, :, None, :]
    outer = (pick(offsets // BS, flags)[:, :, None] * lanes[None]).astype(jnp.float32)[:, :, None, :]

    def siblings(piece):
        return [lax.ppermute(piece, "row", [(i, (i + s) % row) for i in range(row)]) for s in range(1, row)]

    def across(piece, shift):
        return lax.ppermute(piece, "wide", [(i, i ^ shift) for i in range(wide)])

    def others(slot, pieces):
        return [(slot, q + 1, piece) for q, piece in enumerate(pieces)]

    shape = jax.ShapeDtypeStruct((2 * window // LANES, row * nq, window, LANES), jnp.bfloat16)
    prepare = functools.partial(screen, mask)
    mhigh, mlow = mask_amplitudes(inner, amplitudes)
    if line > 1:
        near, cross = across(factors, 1), across(factors, 2)
        high, low = prepare([(0, 0, factors)], shape)
        cross, high, low, mhigh, mlow, places, outer = lax.optimization_barrier(
            (cross, high, low, mhigh, mlow, places, outer))
        last = across(cross, 1)
        early = others(0, siblings(factors)) + [(1, 0, near), (2, 0, cross)]
        s_cross, s_near = siblings(cross), siblings(near)
        high, low = prepare(early, shape, (high, low))
        last, high, low = lax.optimization_barrier((last, high, low))
        contract = functools.partial(contract_pairs, row, col, places, mask, outer)
        s_last = siblings(last)
        ready = [(3, 0, last)] + others(1, s_near) + others(2, s_cross)
        held, high, low = contract(range(nq), False, shifts[:1], ready, mhigh, mlow, high, low)
        far, high, low = contract(range(nq, row * nq), True, shifts[:1], others(3, s_last), mhigh, mlow, high, low, held)
        rest, _, _ = contract(range(row * nq), True, shifts[1:], [], mhigh, mlow, high, low)
        terms = dict(zip(shifts, far + rest))
    else:
        whole = lax.all_gather(factors, "wide", axis=1, tiled=True)
        high, low = prepare([(0, 0, whole)] + others(0, siblings(whole)), shape)
        contract = functools.partial(contract_pairs, row, col, places, mask, outer)
        rest, _, _ = contract(range(row * nq), True, shifts, [], mhigh, mlow, high, low)
        terms = dict(zip(shifts, rest))

    moved = [lax.ppermute(terms[s], "col", [(i, partner(i, s, col)) for i in range(col)]) for s in shifts if s]
    return add_terms(add_terms(terms[0], moved[0], ahead=1 << 24), *moved[1:])


def solution(mesh):
    wide, row, col = (mesh.shape[name] for name in ("wide", "row", "col"))
    return jax.shard_map(
        functools.partial(body, wide, row, col),
        mesh=mesh,
        in_specs=(
            P("wide", None, None),
            P(("row", "col"), "wide", None),
            P("wide", None),
            P("wide", None),
            P(),
        ),
        out_specs=P("wide", ("row", "col"), None),
        check_vma=False,
    )
```

```python
import functools

import jax
import jax.numpy as jnp
from jax import lax
from jax.experimental import pallas as pl
from jax.experimental.pallas import tpu as pltpu
from jax.sharding import PartitionSpec as P

BS = 64
LANES = 128
LINE = 4
VMEM_LIMIT = 40 * 1024 * 1024
VMEM_SPEC = pl.BlockSpec(memory_space=pltpu.VMEM)


def split(value):
    top = value.astype(jnp.bfloat16)
    return top, (value - top.astype(jnp.float32)).astype(jnp.bfloat16)


def partner(index, shift, size):
    if size & (size - 1) == 0:
        return index ^ shift
    return (index + shift) % size


def left_of(rows):
    return lax.broadcasted_iota(jnp.int32, (rows, LANES), 1) < BS


def mask_amplitudes_kernel(weights, amplitudes, high, low):
    pairs, domv, _ = amplitudes.shape
    for p in range(pairs):
        for i in range(domv // BS):
            rows = slice(i * BS, (i + 1) * BS)
            top, rest = split(amplitudes[p, rows, :] * weights[p, i])
            high[p, rows, :] = top
            low[p, rows, :] = rest


def mask_amplitudes(weights, amplitudes):
    shape = jax.ShapeDtypeStruct(amplitudes.shape, jnp.bfloat16)
    return pl.pallas_call(
        mask_amplitudes_kernel,
        name="mask_amplitudes",
        out_shape=[shape] * 2,
        in_specs=[VMEM_SPEC] * 2,
        out_specs=[VMEM_SPEC] * 2,
        compiler_params=pltpu.CompilerParams(vmem_limit_bytes=VMEM_LIMIT),
        cost_estimate=pl.CostEstimate(flops=4 * amplitudes.size, bytes_accessed=8 * amplitudes.size, transcendentals=0),
    )(weights, amplitudes)


def screen_piece(mask, piece, q, slot, high, low):
    nq, rows, window = piece.shape
    tiles = window // LANES
    for h in range(rows // BS):
        block = slot * (rows // BS) + h
        target = slice(block * BS, (block + 1) * BS)
        for t in range(tiles):
            lanes = slice(t * LANES, (t + 1) * LANES)
            for n in range(nq):
                tile = piece[n, h * BS:(h + 1) * BS, lanes] * mask[block, :, lanes]
                for turn, value in ((0, tile), (1, pltpu.roll(tile, BS, 1))):
                    top, rest = split(value)
                    high[turn * tiles + t, q * nq + n, target, :] = top
                    low[turn * tiles + t, q * nq + n, target, :] = rest


def screen_kernel(keys, mask, *refs):
    high, low = refs[-2:]
    for (slot, q), piece in zip(keys, refs):
        screen_piece(mask, piece, q, slot, high, low)


def screen(mask, keyed, shape, held=()):
    keys = [(slot, q) for slot, q, _ in keyed]
    pieces = [piece for _, _, piece in keyed]
    size = sum(piece.size for piece in pieces)
    return pl.pallas_call(
        functools.partial(screen_kernel, keys),
        name="screen_factors",
        out_shape=[shape] * 2,
        in_specs=[VMEM_SPEC] * (1 + len(pieces) + len(held)),
        out_specs=[VMEM_SPEC] * 2,
        input_output_aliases={1 + len(pieces) + i: i for i in range(len(held))},
        compiler_params=pltpu.CompilerParams(vmem_limit_bytes=VMEM_LIMIT),
        cost_estimate=pl.CostEstimate(flops=8 * size, bytes_accessed=12 * size, transcendentals=0),
    )(mask, *pieces, *held)


def pairs_kernel(row, col, factors, last, shifts, places, weights, mhigh, mlow, high, low, *refs):
    count = len(shifts)
    held, outs = refs[:-count], refs[-count:]
    at = places[...]
    pairs, chunk, domv = outs[0].shape
    qs = len(factors)
    size = count * chunk
    blocks = domv // BS
    tiles = domv // LANES
    across = (((1,), (1,)), ((), ()))
    along = (((1,), (0,)), ((), ()))
    dot = functools.partial(lax.dot_general, preferred_element_type=jnp.float32)

    def contract(p):
        def rows_at(n, size):
            return pl.ds(pl.multiple_of(at[0, n * pairs + p], size), size)

        y_spans = [rows_at(i, BS) for i in range(blocks)]
        x_spans = [rows_at(blocks + n, chunk) for n in shifts]
        first = blocks + col
        sources = [(at[0, (first + 2 * j) * pairs + p], at[0, (first + 2 * j + 1) * pairs + p]) for j in range(tiles)]

        def gather(source, q, spans, size):
            return jnp.concatenate([jnp.concatenate([
                jnp.where(left_of(size), source[a, q, span, :], source[b, q, span, :]) for a, b in sources], 1)
                for span in spans], 0)

        yhigh, ylow = (jnp.concatenate([gather(source, q, y_spans, BS) for q in factors], 1) for source in (high, low))
        xhigh, xlow = (jnp.concatenate([gather(source, q, x_spans, chunk) for q in factors], 0) for source in (high, low))
        both = dot(jnp.concatenate([xhigh, xlow], 0), mhigh[p], along)
        halfway = both[:qs * size] + both[qs * size:] + dot(xhigh, mlow[p], along)
        hhigh, hlow = split(jnp.concatenate([halfway[q * size:(q + 1) * size] for q in range(qs)], 1))
        both = dot(jnp.concatenate([hhigh, hlow], 0), yhigh, across)
        total = both[:size] + both[size:] + dot(hhigh, ylow, across)
        for n, (shift, out) in enumerate(zip(shifts, outs)):
            term = total[n * chunk:(n + 1) * chunk]
            if held:
                term += held[n][p]
            out[p] = term * weights[shift, p] if last else term

    for p in range(pairs):
        contract(p)


def contract_pairs(row, col, places, weights, factors, last, shifts, mhigh, mlow, high, low, held=()):
    pairs, domv, _ = mhigh.shape
    chunk = domv // (row * col)
    count = len(shifts)
    return pl.pallas_call(
        functools.partial(pairs_kernel, row, col, factors, last, shifts),
        name="contract_pairs",
        out_shape=[jax.ShapeDtypeStruct((pairs, chunk, domv), jnp.float32)] * count,
        in_specs=[VMEM_SPEC] * (6 + len(held)),
        out_specs=[VMEM_SPEC] * count,
        compiler_params=pltpu.CompilerParams(vmem_limit_bytes=VMEM_LIMIT),
        cost_estimate=pl.CostEstimate(flops=6 * pairs * len(factors) * domv ** 3 * 4 * count // (row * col),
                                      bytes_accessed=8 * high.size, transcendentals=0),
    )(places, weights, mhigh, mlow, high, low, *held)


def add_kernel(*refs):
    total = refs[0][...]
    for ref in refs[1:-1]:
        total += ref[...]
    refs[-1][...] = total


def add_terms(*terms, ahead=0):
    return pl.pallas_call(
        add_kernel,
        name="add_terms",
        out_shape=jax.ShapeDtypeStruct(terms[0].shape, jnp.float32),
        in_specs=[VMEM_SPEC] * len(terms),
        out_specs=VMEM_SPEC,
        compiler_params=pltpu.CompilerParams(vmem_limit_bytes=VMEM_LIMIT),
        cost_estimate=pl.CostEstimate(flops=0, bytes_accessed=ahead + 4 * len(terms) * terms[0].size, transcendentals=0),
    )(*terms)


def body(wide, row, col, amplitudes, factors, domains, domain_mask, block_mask):
    nq, rows, window = factors.shape
    pairs, dom = domains.shape
    z, r, c = lax.axis_index("wide"), lax.axis_index("row"), lax.axis_index("col")
    line = wide if wide == LINE and rows % BS == 0 else 1
    plane = z if line > 1 else 0
    blocks = window // BS
    per_slot = blocks // line
    domv = dom * BS
    tiles = window // LANES
    half = domv // row
    chunk = half // col

    def pick(which, table):
        hits = which[:, None] == jnp.arange(table.shape[0])[None, :]
        return jnp.sum(jnp.where(hits[:, :, None], table[None], 0), axis=1)

    shifts = sorted(range(col), key=lambda s: -bin(s).count("1"))

    blocks_of, flags = domains.T, domain_mask.T
    starts = ((blocks_of // per_slot) ^ plane) * (per_slot * BS) + blocks_of % per_slot * BS
    offsets = r * half + jnp.stack([partner(c, s, col) for s in range(col)]) * chunk
    chosen = pick(offsets // BS, starts) + (offsets % BS)[:, None]
    firsts, seconds = blocks_of[0::2], blocks_of[1::2]
    sources = jnp.stack([firsts % 2 * tiles + firsts // 2, (1 - seconds % 2) * tiles + seconds // 2], 1)
    places = jnp.concatenate([starts, chosen, sources.reshape(-1, pairs)], 0).reshape(1, -1)

    order = jnp.arange(blocks)
    kept = pick(((order // per_slot) ^ plane) * per_slot + order % per_slot, block_mask)
    mask = jnp.repeat(kept, BS, axis=1).astype(jnp.float32)[:, None, :]
    lanes = jnp.repeat(domain_mask, BS, axis=1)
    inner = (domain_mask[:, :, None] * lanes[:, None, :]).astype(jnp.float32)[:, :, None, :]
    outer = (pick(offsets // BS, flags)[:, :, None] * lanes[None]).astype(jnp.float32)[:, :, None, :]

    def siblings(piece):
        return [lax.ppermute(piece, "row", [(i, (i + s) % row) for i in range(row)]) for s in range(1, row)]

    def across(piece, shift):
        return lax.ppermute(piece, "wide", [(i, i ^ shift) for i in range(wide)])

    def others(slot, pieces):
        return [(slot, q + 1, piece) for q, piece in enumerate(pieces)]

    shape = jax.ShapeDtypeStruct((2 * window // LANES, row * nq, window, LANES), jnp.bfloat16)
    prepare = functools.partial(screen, mask)
    mhigh, mlow = mask_amplitudes(inner, amplitudes)
    if line > 1:
        near, cross = across(factors, 1), across(factors, 2)
        high, low = prepare([(0, 0, factors)], shape)
        cross, high, low, mhigh, mlow, places, outer = lax.optimization_barrier(
            (cross, high, low, mhigh, mlow, places, outer))
        last = across(cross, 1)
        early = others(0, siblings(factors)) + [(1, 0, near), (2, 0, cross)]
        s_cross, s_near = siblings(cross), siblings(near)
        high, low = prepare(early, shape, (high, low))
        last, high, low = lax.optimization_barrier((last, high, low))
        contract = functools.partial(contract_pairs, row, col, places, outer)
        s_last = siblings(last)
        high, low = prepare([(3, 0, last)] + others(1, s_near) + others(2, s_cross), shape, (high, low))
        held = contract(range(nq), False, shifts[:1], mhigh, mlow, high, low)
        high, low = prepare(others(3, s_last), shape, (high, low))
        far = contract(range(nq, row * nq), True, shifts[:1], mhigh, mlow, high, low, held)
        far, high, low = lax.optimization_barrier((far, high, low))
        rest = contract(range(row * nq), True, shifts[1:], mhigh, mlow, high, low)
        terms = dict(zip(shifts, far + rest))
    else:
        whole = lax.all_gather(factors, "wide", axis=1, tiled=True)
        high, low = prepare([(0, 0, whole)] + others(0, siblings(whole)), shape)
        contract = functools.partial(contract_pairs, row, col, places, outer)
        rest = contract(range(row * nq), True, shifts, mhigh, mlow, high, low)
        terms = dict(zip(shifts, rest))

    moved = [lax.ppermute(terms[s], "col", [(i, partner(i, s, col)) for i in range(col)]) for s in shifts if s]
    return add_terms(add_terms(terms[0], moved[0], ahead=1 << 24), *moved[1:])


def solution(mesh):
    wide, row, col = (mesh.shape[name] for name in ("wide", "row", "col"))
    return jax.shard_map(
        functools.partial(body, wide, row, col),
        mesh=mesh,
        in_specs=(
            P("wide", None, None),
            P(("row", "col"), "wide", None),
            P("wide", None),
            P("wide", None),
            P(),
        ),
        out_specs=P("wide", ("row", "col"), None),
        check_vma=False,
    )
```

```python
import functools

import jax
import jax.numpy as jnp
from jax import lax
from jax.experimental import pallas as pl
from jax.experimental.pallas import tpu as pltpu
from jax.sharding import PartitionSpec as P

BS = 64
LANES = 128
LINE = 4
VMEM_LIMIT = 40 * 1024 * 1024
VMEM_SPEC = pl.BlockSpec(memory_space=pltpu.VMEM)


def split(value):
    top = value.astype(jnp.bfloat16)
    return top, (value - top.astype(jnp.float32)).astype(jnp.bfloat16)


def partner(index, shift, size):
    if size & (size - 1) == 0:
        return index ^ shift
    return (index + shift) % size


def left_of(rows):
    return lax.broadcasted_iota(jnp.int32, (rows, LANES), 1) < BS


def mask_amplitudes_kernel(weights, amplitudes, high, low):
    pairs, domv, _ = amplitudes.shape
    for p in range(pairs):
        for i in range(domv // BS):
            rows = slice(i * BS, (i + 1) * BS)
            top, rest = split(amplitudes[p, rows, :] * weights[p, i])
            high[p, rows, :] = top
            low[p, rows, :] = rest


def mask_amplitudes(weights, amplitudes):
    shape = jax.ShapeDtypeStruct(amplitudes.shape, jnp.bfloat16)
    return pl.pallas_call(
        mask_amplitudes_kernel,
        name="mask_amplitudes",
        out_shape=[shape] * 2,
        in_specs=[VMEM_SPEC] * 2,
        out_specs=[VMEM_SPEC] * 2,
        compiler_params=pltpu.CompilerParams(vmem_limit_bytes=VMEM_LIMIT),
        cost_estimate=pl.CostEstimate(flops=4 * amplitudes.size, bytes_accessed=8 * amplitudes.size, transcendentals=0),
    )(weights, amplitudes)


def screen_piece(mask, piece, q, slot, packed):
    nq, rows, window = piece.shape
    blocks = window // BS
    left_half = left_of(BS)
    for h in range(rows // BS):
        block = slot * (rows // BS) + h
        target = slice(block * BS, (block + 1) * BS)
        for t in range(window // LANES):
            lanes = slice(t * LANES, (t + 1) * LANES)
            for n in range(nq):
                tile = piece[n, h * BS:(h + 1) * BS, lanes] * mask[block, :, lanes]
                high, low = split(tile)
                turned_high, turned_low = split(pltpu.roll(tile, BS, 1))
                at = q * nq + n
                packed[2 * t, at, target, :] = jnp.where(left_half, high, turned_low)
                packed[2 * t + 1, at, target, :] = jnp.where(left_half, turned_high, low)
                packed[blocks + 2 * t, at, target, :] = jnp.where(left_half, low, turned_high)
                packed[blocks + 2 * t + 1, at, target, :] = jnp.where(left_half, turned_low, high)


def screen_kernel(keys, mask, *refs):
    for (slot, q), piece in zip(keys, refs):
        screen_piece(mask, piece, q, slot, refs[-1])


def screen(mask, keyed, shape, held=()):
    keys = [(slot, q) for slot, q, _ in keyed]
    pieces = [piece for _, _, piece in keyed]
    size = sum(piece.size for piece in pieces)
    return pl.pallas_call(
        functools.partial(screen_kernel, keys),
        name="screen_factors",
        out_shape=shape,
        in_specs=[VMEM_SPEC] * (1 + len(pieces) + len(held)),
        out_specs=VMEM_SPEC,
        input_output_aliases={1 + len(pieces): 0} if held else {},
        compiler_params=pltpu.CompilerParams(vmem_limit_bytes=VMEM_LIMIT),
        cost_estimate=pl.CostEstimate(flops=8 * size, bytes_accessed=12 * size, transcendentals=0),
    )(mask, *pieces, *held)


def pairs_kernel(row, col, factors, last, shifts, places, weights, mhigh, mlow, packed, *refs):
    count = len(shifts)
    held, outs = refs[:-count], refs[-count:]
    at = places[...]
    pairs, chunk, domv = outs[0].shape
    qs = len(factors)
    size = count * chunk
    blocks = domv // BS
    turned = packed.shape[0] // 2
    across = (((1,), (1,)), ((), ()))
    along = (((1,), (0,)), ((), ()))
    dot = functools.partial(lax.dot_general, preferred_element_type=jnp.float32)

    def contract(p):
        def rows_at(n, size):
            return pl.ds(pl.multiple_of(at[0, n * pairs + p], size), size)

        y_spans = [rows_at(i, BS) for i in range(blocks)]
        x_spans = [rows_at(blocks + n, chunk) for n in shifts]
        columns = [at[0, (blocks + col + i) * pairs + p] for i in range(blocks)]

        def x_part(q, low):
            return jnp.concatenate([jnp.concatenate([jnp.where(
                left_of(chunk), packed[columns[i] + low * turned, q, span, :], packed[columns[i + 1] + (1 - low) * turned, q, span, :])
                for i in range(0, blocks, 2)], 1) for span in x_spans], 0)

        xhigh, xlow = (jnp.concatenate([x_part(q, low) for q in factors], 0) for low in range(2))
        both = dot(jnp.concatenate([xhigh, xlow], 0), mhigh[p], along)
        halfway = both[:qs * size] + both[qs * size:] + dot(xhigh, mlow[p], along)

        doubled = []
        for q in range(qs):
            for j in range(domv // LANES):
                tile = halfway[q * size:(q + 1) * size, j * LANES:(j + 1) * LANES]
                other = pltpu.roll(tile, BS, 1)
                doubled += [jnp.where(left_of(size), tile, other), jnp.where(left_of(size), other, tile)]
        hhigh, hlow = split(jnp.concatenate(doubled, 1))
        y = jnp.concatenate([jnp.concatenate([packed[column, q, span, :] for q in factors for column in columns], 1)
                             for span in y_spans], 0)
        both = dot(jnp.concatenate([hhigh, hlow], 0), y, across)
        total = both[:size] + both[size:]
        for n, (shift, out) in enumerate(zip(shifts, outs)):
            term = total[n * chunk:(n + 1) * chunk]
            if held:
                term += held[n][p]
            out[p] = term * weights[shift, p] if last else term

    for p in range(pairs):
        contract(p)


def contract_pairs(row, col, places, weights, factors, last, shifts, mhigh, mlow, packed, held=()):
    pairs, domv, _ = mhigh.shape
    chunk = domv // (row * col)
    count = len(shifts)
    return pl.pallas_call(
        functools.partial(pairs_kernel, row, col, factors, last, shifts),
        name="contract_pairs",
        out_shape=[jax.ShapeDtypeStruct((pairs, chunk, domv), jnp.float32)] * count,
        in_specs=[VMEM_SPEC] * (5 + len(held)),
        out_specs=[VMEM_SPEC] * count,
        compiler_params=pltpu.CompilerParams(vmem_limit_bytes=VMEM_LIMIT),
        cost_estimate=pl.CostEstimate(flops=6 * pairs * len(factors) * domv ** 3 * 4 * count // (row * col),
                                      bytes_accessed=4 * packed.size, transcendentals=0),
    )(places, weights, mhigh, mlow, packed, *held)


def add_kernel(*refs):
    total = refs[0][...]
    for ref in refs[1:-1]:
        total += ref[...]
    refs[-1][...] = total


def add_terms(*terms, ahead=0):
    return pl.pallas_call(
        add_kernel,
        name="add_terms",
        out_shape=jax.ShapeDtypeStruct(terms[0].shape, jnp.float32),
        in_specs=[VMEM_SPEC] * len(terms),
        out_specs=VMEM_SPEC,
        compiler_params=pltpu.CompilerParams(vmem_limit_bytes=VMEM_LIMIT),
        cost_estimate=pl.CostEstimate(flops=0, bytes_accessed=ahead + 4 * len(terms) * terms[0].size, transcendentals=0),
    )(*terms)


def body(wide, row, col, amplitudes, factors, domains, domain_mask, block_mask):
    nq, rows, window = factors.shape
    pairs, dom = domains.shape
    z, r, c = lax.axis_index("wide"), lax.axis_index("row"), lax.axis_index("col")
    line = wide if wide == LINE and rows % BS == 0 else 1
    plane = z if line > 1 else 0
    blocks = window // BS
    per_slot = blocks // line
    domv = dom * BS
    half = domv // row
    chunk = half // col

    def pick(which, table):
        hits = which[:, None] == jnp.arange(table.shape[0])[None, :]
        return jnp.sum(jnp.where(hits[:, :, None], table[None], 0), axis=1)

    shifts = sorted(range(col), key=lambda s: -bin(s).count("1"))

    blocks_of, flags = domains.T, domain_mask.T
    starts = ((blocks_of // per_slot) ^ plane) * (per_slot * BS) + blocks_of % per_slot * BS
    offsets = r * half + jnp.stack([partner(c, s, col) for s in range(col)]) * chunk
    chosen = pick(offsets // BS, starts) + (offsets % BS)[:, None]
    places = jnp.concatenate([starts, chosen, blocks_of], 0).reshape(1, -1)

    order = jnp.arange(blocks)
    kept = pick(((order // per_slot) ^ plane) * per_slot + order % per_slot, block_mask)
    mask = jnp.repeat(kept, BS, axis=1).astype(jnp.float32)[:, None, :]
    lanes = jnp.repeat(domain_mask, BS, axis=1)
    inner = (domain_mask[:, :, None] * lanes[:, None, :]).astype(jnp.float32)[:, :, None, :]
    outer = (pick(offsets // BS, flags)[:, :, None] * lanes[None]).astype(jnp.float32)[:, :, None, :]

    def siblings(piece):
        return [lax.ppermute(piece, "row", [(i, (i + s) % row) for i in range(row)]) for s in range(1, row)]

    def across(piece, shift):
        return lax.ppermute(piece, "wide", [(i, i ^ shift) for i in range(wide)])

    def others(slot, pieces):
        return [(slot, q + 1, piece) for q, piece in enumerate(pieces)]

    shape = jax.ShapeDtypeStruct((2 * blocks, row * nq, window, LANES), jnp.bfloat16)
    prepare = functools.partial(screen, mask)
    mhigh, mlow = mask_amplitudes(inner, amplitudes)
    if line > 1:
        near, cross = across(factors, 1), across(factors, 2)
        packed = prepare([(0, 0, factors)], shape)
        cross, packed, mhigh, mlow, places, outer = lax.optimization_barrier(
            (cross, packed, mhigh, mlow, places, outer))
        last = across(cross, 1)
        early = others(0, siblings(factors)) + [(1, 0, near), (2, 0, cross)]
        s_cross, s_near = siblings(cross), siblings(near)
        packed = prepare(early, shape, (packed,))
        last, packed = lax.optimization_barrier((last, packed))
        contract = functools.partial(contract_pairs, row, col, places, outer)
        s_last = siblings(last)
        packed = prepare([(3, 0, last)] + others(1, s_near) + others(2, s_cross), shape, (packed,))
        held = contract(range(nq), False, shifts[:1], mhigh, mlow, packed)
        packed = prepare(others(3, s_last), shape, (packed,))
        far = contract(range(nq, row * nq), True, shifts[:1], mhigh, mlow, packed, held)
        _, packed = lax.optimization_barrier((far, packed))
        rest = contract(range(row * nq), True, shifts[1:], mhigh, mlow, packed)
        terms = dict(zip(shifts, far + rest))
    else:
        whole = lax.all_gather(factors, "wide", axis=1, tiled=True)
        packed = prepare([(0, 0, whole)] + others(0, siblings(whole)), shape)
        contract = functools.partial(contract_pairs, row, col, places, outer)
        rest = contract(range(row * nq), True, shifts, mhigh, mlow, packed)
        terms = dict(zip(shifts, rest))

    moved = [lax.ppermute(terms[s], "col", [(i, partner(i, s, col)) for i in range(col)]) for s in shifts if s]
    return add_terms(add_terms(terms[0], moved[0], ahead=1 << 24), *moved[1:])


def solution(mesh):
    wide, row, col = (mesh.shape[name] for name in ("wide", "row", "col"))
    return jax.shard_map(
        functools.partial(body, wide, row, col),
        mesh=mesh,
        in_specs=(
            P("wide", None, None),
            P(("row", "col"), "wide", None),
            P("wide", None),
            P("wide", None),
            P(),
        ),
        out_specs=P("wide", ("row", "col"), None),
        check_vma=False,
    )
```

```python
import functools

import jax
import jax.numpy as jnp
from jax import lax
from jax.experimental import pallas as pl
from jax.experimental.pallas import tpu as pltpu
from jax.sharding import PartitionSpec as P

BS = 64
LANES = 128
LINE = 4
VMEM_LIMIT = 40 * 1024 * 1024
VMEM_SPEC = pl.BlockSpec(memory_space=pltpu.VMEM)


def split(value):
    top = value.astype(jnp.bfloat16)
    return top, (value - top.astype(jnp.float32)).astype(jnp.bfloat16)


def partner(index, shift, size):
    if size & (size - 1) == 0:
        return index ^ shift
    return (index + shift) % size


def left_of(rows):
    return lax.broadcasted_iota(jnp.int32, (rows, LANES), 1) < BS


def mask_amplitudes_kernel(weights, amplitudes, high, low):
    pairs, domv, _ = amplitudes.shape
    for p in range(pairs):
        for i in range(domv // BS):
            rows = slice(i * BS, (i + 1) * BS)
            top, rest = split(amplitudes[p, rows, :] * weights[p, i])
            high[p, rows, :] = top
            low[p, rows, :] = rest


def mask_amplitudes(weights, amplitudes):
    shape = jax.ShapeDtypeStruct(amplitudes.shape, jnp.bfloat16)
    return pl.pallas_call(
        mask_amplitudes_kernel,
        name="mask_amplitudes",
        out_shape=[shape] * 2,
        in_specs=[VMEM_SPEC] * 2,
        out_specs=[VMEM_SPEC] * 2,
        compiler_params=pltpu.CompilerParams(vmem_limit_bytes=VMEM_LIMIT),
        cost_estimate=pl.CostEstimate(flops=4 * amplitudes.size, bytes_accessed=8 * amplitudes.size, transcendentals=0),
    )(weights, amplitudes)


def screen_piece(mask, piece, q, slot, high, low):
    nq, rows, window = piece.shape
    tiles = window // LANES
    for h in range(rows // BS):
        block = slot * (rows // BS) + h
        target = slice(block * BS, (block + 1) * BS)
        for t in range(tiles):
            lanes = slice(t * LANES, (t + 1) * LANES)
            for n in range(nq):
                tile = piece[n, h * BS:(h + 1) * BS, lanes] * mask[block, :, lanes]
                for turn, value in ((0, tile), (1, pltpu.roll(tile, BS, 1))):
                    top, rest = split(value)
                    high[turn * tiles + t, q * nq + n, target, :] = top
                    low[turn * tiles + t, q * nq + n, target, :] = rest


def screen_kernel(keys, mask, *refs):
    high, low = refs[-2:]
    for (slot, q), piece in zip(keys, refs):
        screen_piece(mask, piece, q, slot, high, low)


def screen(mask, keyed, shape, held=()):
    keys = [(slot, q) for slot, q, _ in keyed]
    pieces = [piece for _, _, piece in keyed]
    size = sum(piece.size for piece in pieces)
    return pl.pallas_call(
        functools.partial(screen_kernel, keys),
        name="screen_factors",
        out_shape=[shape] * 2,
        in_specs=[VMEM_SPEC] * (1 + len(pieces) + len(held)),
        out_specs=[VMEM_SPEC] * 2,
        input_output_aliases={1 + len(pieces) + i: i for i in range(len(held))},
        compiler_params=pltpu.CompilerParams(vmem_limit_bytes=VMEM_LIMIT),
        cost_estimate=pl.CostEstimate(flops=8 * size, bytes_accessed=12 * size, transcendentals=0),
    )(mask, *pieces, *held)


def pairs_kernel(row, col, factors, last, shifts, places, weights, mhigh, mlow, high, low, *refs):
    count = len(shifts)
    held, outs = refs[:-count], refs[-count:]
    at = places[...]
    pairs, chunk, domv = outs[0].shape
    qs = len(factors)
    size = count * chunk
    blocks = domv // BS
    tiles = domv // LANES
    across = (((1,), (1,)), ((), ()))
    along = (((1,), (0,)), ((), ()))
    dot = functools.partial(lax.dot_general, preferred_element_type=jnp.float32)

    def rows_at(n, p, size):
        return pl.ds(pl.multiple_of(at[0, n * pairs + p], size), size)

    def gather(source, p, q, spans, size):
        first = blocks + col
        sources = [(at[0, (first + 2 * j) * pairs + p], at[0, (first + 2 * j + 1) * pairs + p]) for j in range(tiles)]
        return jnp.concatenate([jnp.concatenate([
            jnp.where(left_of(size), source[a, q, span, :], source[b, q, span, :]) for a, b in sources], 1)
            for span in spans], 0)

    def first_product(p):
        spans = [rows_at(blocks + n, p, chunk) for n in shifts]
        xhigh, xlow = (jnp.concatenate([gather(source, p, q, spans, chunk) for q in factors], 0) for source in (high, low))
        both = dot(jnp.concatenate([xhigh, xlow], 0), mhigh[p], along)
        halfway = both[:qs * size] + both[qs * size:] + dot(xhigh, mlow[p], along)
        return split(jnp.concatenate([halfway[q * size:(q + 1) * size] for q in range(qs)], 1))

    def second_product(p, hhigh, hlow):
        spans = [rows_at(i, p, BS) for i in range(blocks)]
        yhigh, ylow = (jnp.concatenate([gather(source, p, q, spans, BS) for q in factors], 1) for source in (high, low))
        both = dot(jnp.concatenate([hhigh, hlow], 0), yhigh, across)
        total = both[:size] + both[size:] + dot(hhigh, ylow, across)
        for n, (shift, out) in enumerate(zip(shifts, outs)):
            term = total[n * chunk:(n + 1) * chunk]
            if held:
                term += held[n][p]
            out[p] = term * weights[shift, p] if last else term

    together = pairs if count == 1 else 1
    for start in range(0, pairs, together):
        group = range(start, start + together)
        parts = [first_product(p) for p in group]
        for p, (hhigh, hlow) in zip(group, parts):
            second_product(p, hhigh, hlow)


def contract_pairs(row, col, places, weights, factors, last, shifts, mhigh, mlow, high, low, held=()):
    pairs, domv, _ = mhigh.shape
    chunk = domv // (row * col)
    count = len(shifts)
    return pl.pallas_call(
        functools.partial(pairs_kernel, row, col, factors, last, shifts),
        name="contract_pairs",
        out_shape=[jax.ShapeDtypeStruct((pairs, chunk, domv), jnp.float32)] * count,
        in_specs=[VMEM_SPEC] * (6 + len(held)),
        out_specs=[VMEM_SPEC] * count,
        compiler_params=pltpu.CompilerParams(vmem_limit_bytes=VMEM_LIMIT),
        cost_estimate=pl.CostEstimate(flops=6 * pairs * len(factors) * domv ** 3 * 4 * count // (row * col),
                                      bytes_accessed=8 * high.size, transcendentals=0),
    )(places, weights, mhigh, mlow, high, low, *held)


def add_kernel(*refs):
    total = refs[0][...]
    for ref in refs[1:-1]:
        total += ref[...]
    refs[-1][...] = total


def add_terms(*terms, ahead=0):
    return pl.pallas_call(
        add_kernel,
        name="add_terms",
        out_shape=jax.ShapeDtypeStruct(terms[0].shape, jnp.float32),
        in_specs=[VMEM_SPEC] * len(terms),
        out_specs=VMEM_SPEC,
        compiler_params=pltpu.CompilerParams(vmem_limit_bytes=VMEM_LIMIT),
        cost_estimate=pl.CostEstimate(flops=0, bytes_accessed=ahead + 4 * len(terms) * terms[0].size, transcendentals=0),
    )(*terms)


def body(wide, row, col, amplitudes, factors, domains, domain_mask, block_mask):
    nq, rows, window = factors.shape
    pairs, dom = domains.shape
    z, r, c = lax.axis_index("wide"), lax.axis_index("row"), lax.axis_index("col")
    line = wide if wide == LINE and rows % BS == 0 else 1
    plane = z if line > 1 else 0
    blocks = window // BS
    per_slot = blocks // line
    domv = dom * BS
    tiles = window // LANES
    half = domv // row
    chunk = half // col

    def pick(which, table):
        hits = which[:, None] == jnp.arange(table.shape[0])[None, :]
        return jnp.sum(jnp.where(hits[:, :, None], table[None], 0), axis=1)

    shifts = sorted(range(col), key=lambda s: -bin(s).count("1"))

    blocks_of, flags = domains.T, domain_mask.T
    starts = ((blocks_of // per_slot) ^ plane) * (per_slot * BS) + blocks_of % per_slot * BS
    offsets = r * half + jnp.stack([partner(c, s, col) for s in range(col)]) * chunk
    chosen = pick(offsets // BS, starts) + (offsets % BS)[:, None]
    firsts, seconds = blocks_of[0::2], blocks_of[1::2]
    sources = jnp.stack([firsts % 2 * tiles + firsts // 2, (1 - seconds % 2) * tiles + seconds // 2], 1)
    places = jnp.concatenate([starts, chosen, sources.reshape(-1, pairs)], 0).reshape(1, -1)

    order = jnp.arange(blocks)
    kept = pick(((order // per_slot) ^ plane) * per_slot + order % per_slot, block_mask)
    mask = jnp.repeat(kept, BS, axis=1).astype(jnp.float32)[:, None, :]
    lanes = jnp.repeat(domain_mask, BS, axis=1)
    inner = (domain_mask[:, :, None] * lanes[:, None, :]).astype(jnp.float32)[:, :, None, :]
    outer = (pick(offsets // BS, flags)[:, :, None] * lanes[None]).astype(jnp.float32)[:, :, None, :]

    def siblings(piece):
        return [lax.ppermute(piece, "row", [(i, (i + s) % row) for i in range(row)]) for s in range(1, row)]

    def across(piece, shift):
        return lax.ppermute(piece, "wide", [(i, i ^ shift) for i in range(wide)])

    def others(slot, pieces):
        return [(slot, q + 1, piece) for q, piece in enumerate(pieces)]

    shape = jax.ShapeDtypeStruct((2 * window // LANES, row * nq, window, LANES), jnp.bfloat16)
    prepare = functools.partial(screen, mask)
    mhigh, mlow = mask_amplitudes(inner, amplitudes)
    if line > 1:
        near, cross = across(factors, 1), across(factors, 2)
        high, low = prepare([(0, 0, factors)], shape)
        cross, high, low, mhigh, mlow, places, outer = lax.optimization_barrier(
            (cross, high, low, mhigh, mlow, places, outer))
        last = across(cross, 1)
        early = others(0, siblings(factors)) + [(1, 0, near), (2, 0, cross)]
        s_cross, s_near = siblings(cross), siblings(near)
        high, low = prepare(early, shape, (high, low))
        last, high, low = lax.optimization_barrier((last, high, low))
        contract = functools.partial(contract_pairs, row, col, places, outer)
        s_last = siblings(last)
        high, low = prepare([(3, 0, last)] + others(1, s_near) + others(2, s_cross), shape, (high, low))
        held = contract(range(nq), False, shifts[:1], mhigh, mlow, high, low)
        high, low = prepare(others(3, s_last), shape, (high, low))
        far = contract(range(nq, row * nq), True, shifts[:1], mhigh, mlow, high, low, held)
        far, high, low = lax.optimization_barrier((far, high, low))
        rest = contract(range(row * nq), True, shifts[1:], mhigh, mlow, high, low)
        terms = dict(zip(shifts, far + rest))
    else:
        whole = lax.all_gather(factors, "wide", axis=1, tiled=True)
        high, low = prepare([(0, 0, whole)] + others(0, siblings(whole)), shape)
        contract = functools.partial(contract_pairs, row, col, places, outer)
        rest = contract(range(row * nq), True, shifts, mhigh, mlow, high, low)
        terms = dict(zip(shifts, rest))

    moved = [lax.ppermute(terms[s], "col", [(i, partner(i, s, col)) for i in range(col)]) for s in shifts if s]
    return add_terms(add_terms(terms[0], moved[0], ahead=1 << 24), *moved[1:])


def solution(mesh):
    wide, row, col = (mesh.shape[name] for name in ("wide", "row", "col"))
    return jax.shard_map(
        functools.partial(body, wide, row, col),
        mesh=mesh,
        in_specs=(
            P("wide", None, None),
            P(("row", "col"), "wide", None),
            P("wide", None),
            P("wide", None),
            P(),
        ),
        out_specs=P("wide", ("row", "col"), None),
        check_vma=False,
    )
```

```python
import functools

import jax
import jax.numpy as jnp
from jax import lax
from jax.experimental import pallas as pl
from jax.experimental.pallas import tpu as pltpu
from jax.sharding import PartitionSpec as P

BS = 64
LANES = 128
LINE = 4
VMEM_LIMIT = 40 * 1024 * 1024
VMEM_SPEC = pl.BlockSpec(memory_space=pltpu.VMEM)


def split(value):
    top = value.astype(jnp.bfloat16)
    return top, (value - top.astype(jnp.float32)).astype(jnp.bfloat16)


def partner(index, shift, size):
    if size & (size - 1) == 0:
        return index ^ shift
    return (index + shift) % size


def left_of(rows):
    return lax.broadcasted_iota(jnp.int32, (rows, LANES), 1) < BS


def mask_amplitudes_kernel(weights, amplitudes, high, low):
    pairs, domv, _ = amplitudes.shape
    for p in range(pairs):
        for i in range(domv // BS):
            rows = slice(i * BS, (i + 1) * BS)
            top, rest = split(amplitudes[p, rows, :] * weights[p, i])
            high[p, rows, :] = top
            low[p, rows, :] = rest


def mask_amplitudes(weights, amplitudes):
    shape = jax.ShapeDtypeStruct(amplitudes.shape, jnp.bfloat16)
    return pl.pallas_call(
        mask_amplitudes_kernel,
        name="mask_amplitudes",
        out_shape=[shape] * 2,
        in_specs=[VMEM_SPEC] * 2,
        out_specs=[VMEM_SPEC] * 2,
        compiler_params=pltpu.CompilerParams(vmem_limit_bytes=VMEM_LIMIT),
        cost_estimate=pl.CostEstimate(flops=4 * amplitudes.size, bytes_accessed=8 * amplitudes.size, transcendentals=0),
    )(weights, amplitudes)


def screen_piece(mask, piece, q, slot, high, low):
    nq, rows, window = piece.shape
    tiles = window // LANES
    for h in range(rows // BS):
        block = slot * (rows // BS) + h
        target = slice(block * BS, (block + 1) * BS)
        for t in range(tiles):
            lanes = slice(t * LANES, (t + 1) * LANES)
            for n in range(nq):
                tile = piece[n, h * BS:(h + 1) * BS, lanes] * mask[block, :, lanes]
                for turn, value in ((0, tile), (1, pltpu.roll(tile, BS, 1))):
                    top, rest = split(value)
                    high[turn * tiles + t, q * nq + n, target, :] = top
                    low[turn * tiles + t, q * nq + n, target, :] = rest


def screen_kernel(keys, mask, *refs):
    high, low = refs[-2:]
    for (slot, q), piece in zip(keys, refs):
        screen_piece(mask, piece, q, slot, high, low)


def screen(mask, keyed, shape, held=()):
    keys = [(slot, q) for slot, q, _ in keyed]
    pieces = [piece for _, _, piece in keyed]
    size = sum(piece.size for piece in pieces)
    return pl.pallas_call(
        functools.partial(screen_kernel, keys),
        name="screen_factors",
        out_shape=[shape] * 2,
        in_specs=[VMEM_SPEC] * (1 + len(pieces) + len(held)),
        out_specs=[VMEM_SPEC] * 2,
        input_output_aliases={1 + len(pieces) + i: i for i in range(len(held))},
        compiler_params=pltpu.CompilerParams(vmem_limit_bytes=VMEM_LIMIT),
        cost_estimate=pl.CostEstimate(flops=8 * size, bytes_accessed=12 * size, transcendentals=0),
    )(mask, *pieces, *held)


def pairs_kernel(row, col, factors, last, shifts, places, weights, mhigh, mlow, high, low, *refs):
    count = len(shifts)
    held, outs = refs[:-count], refs[-count:]
    at = places[...]
    pairs, chunk, domv = outs[0].shape
    qs = len(factors)
    size = count * chunk
    blocks = domv // BS
    tiles = domv // LANES
    across = (((1,), (1,)), ((), ()))
    along = (((1,), (0,)), ((), ()))
    dot = functools.partial(lax.dot_general, preferred_element_type=jnp.float32)

    def rows_at(n, p, size):
        return pl.ds(pl.multiple_of(at[0, n * pairs + p], size), size)

    def gather(source, p, q, spans, size):
        first = blocks + col
        sources = [(at[0, (first + 2 * j) * pairs + p], at[0, (first + 2 * j + 1) * pairs + p]) for j in range(tiles)]
        return jnp.concatenate([jnp.concatenate([
            jnp.where(left_of(size), source[a, q, span, :], source[b, q, span, :]) for a, b in sources], 1)
            for span in spans], 0)

    def first_product(p):
        spans = [rows_at(blocks + n, p, chunk) for n in shifts]
        xhigh, xlow = (jnp.concatenate([gather(source, p, q, spans, chunk) for q in factors], 0) for source in (high, low))
        both = dot(jnp.concatenate([xhigh, xlow], 0), mhigh[p], along)
        halfway = both[:qs * size] + both[qs * size:] + dot(xhigh, mlow[p], along)
        return split(jnp.concatenate([halfway[q * size:(q + 1) * size] for q in range(qs)], 1))

    def second_product(p, hhigh, hlow):
        spans = [rows_at(i, p, BS) for i in range(blocks)]
        yhigh, ylow = (jnp.concatenate([gather(source, p, q, spans, BS) for q in factors], 1) for source in (high, low))
        both = dot(jnp.concatenate([hhigh, hlow], 0), yhigh, across)
        total = both[:size] + both[size:] + dot(hhigh, ylow, across)
        for n, (shift, out) in enumerate(zip(shifts, outs)):
            term = total[n * chunk:(n + 1) * chunk]
            if held:
                term += held[n][p]
            out[p] = term * weights[shift, p] if last else term

    together = pairs if count == 1 else max(1, pairs // 2)
    for start in range(0, pairs, together):
        group = range(start, min(start + together, pairs))
        parts = [first_product(p) for p in group]
        for p, (hhigh, hlow) in zip(group, parts):
            second_product(p, hhigh, hlow)


def contract_pairs(row, col, places, weights, factors, last, shifts, mhigh, mlow, high, low, held=()):
    pairs, domv, _ = mhigh.shape
    chunk = domv // (row * col)
    count = len(shifts)
    return pl.pallas_call(
        functools.partial(pairs_kernel, row, col, factors, last, shifts),
        name="contract_pairs",
        out_shape=[jax.ShapeDtypeStruct((pairs, chunk, domv), jnp.float32)] * count,
        in_specs=[VMEM_SPEC] * (6 + len(held)),
        out_specs=[VMEM_SPEC] * count,
        compiler_params=pltpu.CompilerParams(vmem_limit_bytes=VMEM_LIMIT),
        cost_estimate=pl.CostEstimate(flops=6 * pairs * len(factors) * domv ** 3 * 4 * count // (row * col),
                                      bytes_accessed=8 * high.size, transcendentals=0),
    )(places, weights, mhigh, mlow, high, low, *held)


def add_kernel(*refs):
    total = refs[0][...]
    for ref in refs[1:-1]:
        total += ref[...]
    refs[-1][...] = total


def add_terms(*terms, ahead=0):
    return pl.pallas_call(
        add_kernel,
        name="add_terms",
        out_shape=jax.ShapeDtypeStruct(terms[0].shape, jnp.float32),
        in_specs=[VMEM_SPEC] * len(terms),
        out_specs=VMEM_SPEC,
        compiler_params=pltpu.CompilerParams(vmem_limit_bytes=VMEM_LIMIT),
        cost_estimate=pl.CostEstimate(flops=0, bytes_accessed=ahead + 4 * len(terms) * terms[0].size, transcendentals=0),
    )(*terms)


def body(wide, row, col, amplitudes, factors, domains, domain_mask, block_mask):
    nq, rows, window = factors.shape
    pairs, dom = domains.shape
    z, r, c = lax.axis_index("wide"), lax.axis_index("row"), lax.axis_index("col")
    line = wide if wide == LINE and rows % BS == 0 else 1
    plane = z if line > 1 else 0
    blocks = window // BS
    per_slot = blocks // line
    domv = dom * BS
    tiles = window // LANES
    half = domv // row
    chunk = half // col

    def pick(which, table):
        hits = which[:, None] == jnp.arange(table.shape[0])[None, :]
        return jnp.sum(jnp.where(hits[:, :, None], table[None], 0), axis=1)

    shifts = sorted(range(col), key=lambda s: -bin(s).count("1"))

    blocks_of, flags = domains.T, domain_mask.T
    starts = ((blocks_of // per_slot) ^ plane) * (per_slot * BS) + blocks_of % per_slot * BS
    offsets = r * half + jnp.stack([partner(c, s, col) for s in range(col)]) * chunk
    chosen = pick(offsets // BS, starts) + (offsets % BS)[:, None]
    firsts, seconds = blocks_of[0::2], blocks_of[1::2]
    sources = jnp.stack([firsts % 2 * tiles + firsts // 2, (1 - seconds % 2) * tiles + seconds // 2], 1)
    places = jnp.concatenate([starts, chosen, sources.reshape(-1, pairs)], 0).reshape(1, -1)

    order = jnp.arange(blocks)
    kept = pick(((order // per_slot) ^ plane) * per_slot + order % per_slot, block_mask)
    mask = jnp.repeat(kept, BS, axis=1).astype(jnp.float32)[:, None, :]
    lanes = jnp.repeat(domain_mask, BS, axis=1)
    inner = (domain_mask[:, :, None] * lanes[:, None, :]).astype(jnp.float32)[:, :, None, :]
    outer = (pick(offsets // BS, flags)[:, :, None] * lanes[None]).astype(jnp.float32)[:, :, None, :]

    def siblings(piece):
        return [lax.ppermute(piece, "row", [(i, (i + s) % row) for i in range(row)]) for s in range(1, row)]

    def across(piece, shift):
        return lax.ppermute(piece, "wide", [(i, i ^ shift) for i in range(wide)])

    def others(slot, pieces):
        return [(slot, q + 1, piece) for q, piece in enumerate(pieces)]

    shape = jax.ShapeDtypeStruct((2 * window // LANES, row * nq, window, LANES), jnp.bfloat16)
    prepare = functools.partial(screen, mask)
    mhigh, mlow = mask_amplitudes(inner, amplitudes)
    if line > 1:
        near, cross = across(factors, 1), across(factors, 2)
        high, low = prepare([(0, 0, factors)], shape)
        cross, high, low, mhigh, mlow, places, outer = lax.optimization_barrier(
            (cross, high, low, mhigh, mlow, places, outer))
        last = across(cross, 1)
        early = others(0, siblings(factors)) + [(1, 0, near), (2, 0, cross)]
        s_cross, s_near = siblings(cross), siblings(near)
        high, low = prepare(early, shape, (high, low))
        last, high, low = lax.optimization_barrier((last, high, low))
        contract = functools.partial(contract_pairs, row, col, places, outer)
        s_last = siblings(last)
        high, low = prepare([(3, 0, last)] + others(1, s_near) + others(2, s_cross), shape, (high, low))
        held = contract(range(nq), False, shifts[:1], mhigh, mlow, high, low)
        high, low = prepare(others(3, s_last), shape, (high, low))
        far = contract(range(nq, row * nq), True, shifts[:1], mhigh, mlow, high, low, held)
        far, high, low = lax.optimization_barrier((far, high, low))
        rest = contract(range(row * nq), True, shifts[1:], mhigh, mlow, high, low)
        terms = dict(zip(shifts, far + rest))
    else:
        whole = lax.all_gather(factors, "wide", axis=1, tiled=True)
        high, low = prepare([(0, 0, whole)] + others(0, siblings(whole)), shape)
        contract = functools.partial(contract_pairs, row, col, places, outer)
        rest = contract(range(row * nq), True, shifts, mhigh, mlow, high, low)
        terms = dict(zip(shifts, rest))

    moved = [lax.ppermute(terms[s], "col", [(i, partner(i, s, col)) for i in range(col)]) for s in shifts if s]
    return add_terms(add_terms(terms[0], moved[0], ahead=1 << 24), *moved[1:])


def solution(mesh):
    wide, row, col = (mesh.shape[name] for name in ("wide", "row", "col"))
    return jax.shard_map(
        functools.partial(body, wide, row, col),
        mesh=mesh,
        in_specs=(
            P("wide", None, None),
            P(("row", "col"), "wide", None),
            P("wide", None),
            P("wide", None),
            P(),
        ),
        out_specs=P("wide", ("row", "col"), None),
        check_vma=False,
    )
```

```python
import functools

import jax
import jax.numpy as jnp
from jax import lax
from jax.experimental import pallas as pl
from jax.experimental.pallas import tpu as pltpu
from jax.sharding import PartitionSpec as P

BS = 64
LANES = 128
LINE = 4
VMEM_LIMIT = 40 * 1024 * 1024
VMEM_SPEC = pl.BlockSpec(memory_space=pltpu.VMEM)


def split(value):
    top = value.astype(jnp.bfloat16)
    return top, (value - top.astype(jnp.float32)).astype(jnp.bfloat16)


def partner(index, shift, size):
    if size & (size - 1) == 0:
        return index ^ shift
    return (index + shift) % size


def left_of(rows):
    return lax.broadcasted_iota(jnp.int32, (rows, LANES), 1) < BS


def mask_amplitudes_kernel(weights, amplitudes, high, low):
    pairs, domv, _ = amplitudes.shape
    for p in range(pairs):
        for i in range(domv // BS):
            rows = slice(i * BS, (i + 1) * BS)
            top, rest = split(amplitudes[p, rows, :] * weights[p, i])
            high[p, rows, :] = top
            low[p, rows, :] = rest


def mask_amplitudes(weights, amplitudes):
    shape = jax.ShapeDtypeStruct(amplitudes.shape, jnp.bfloat16)
    return pl.pallas_call(
        mask_amplitudes_kernel,
        name="mask_amplitudes",
        out_shape=[shape] * 2,
        in_specs=[VMEM_SPEC] * 2,
        out_specs=[VMEM_SPEC] * 2,
        compiler_params=pltpu.CompilerParams(vmem_limit_bytes=VMEM_LIMIT),
        cost_estimate=pl.CostEstimate(flops=4 * amplitudes.size, bytes_accessed=8 * amplitudes.size, transcendentals=0),
    )(weights, amplitudes)


def screen_piece(mask, piece, q, slot, high, low):
    nq, rows, window = piece.shape
    tiles = window // LANES
    for h in range(rows // BS):
        block = slot * (rows // BS) + h
        target = slice(block * BS, (block + 1) * BS)
        for t in range(tiles):
            lanes = slice(t * LANES, (t + 1) * LANES)
            for n in range(nq):
                tile = piece[n, h * BS:(h + 1) * BS, lanes] * mask[block, :, lanes]
                for turn, value in ((0, tile), (1, pltpu.roll(tile, BS, 1))):
                    top, rest = split(value)
                    high[turn * tiles + t, q * nq + n, target, :] = top
                    low[turn * tiles + t, q * nq + n, target, :] = rest


def screen_kernel(keys, mask, *refs):
    high, low = refs[-2:]
    for (slot, q), piece in zip(keys, refs):
        screen_piece(mask, piece, q, slot, high, low)


def screen(mask, keyed, shape, held=()):
    keys = [(slot, q) for slot, q, _ in keyed]
    pieces = [piece for _, _, piece in keyed]
    size = sum(piece.size for piece in pieces)
    return pl.pallas_call(
        functools.partial(screen_kernel, keys),
        name="screen_factors",
        out_shape=[shape] * 2,
        in_specs=[VMEM_SPEC] * (1 + len(pieces) + len(held)),
        out_specs=[VMEM_SPEC] * 2,
        input_output_aliases={1 + len(pieces) + i: i for i in range(len(held))},
        compiler_params=pltpu.CompilerParams(vmem_limit_bytes=VMEM_LIMIT),
        cost_estimate=pl.CostEstimate(flops=8 * size, bytes_accessed=12 * size, transcendentals=0),
    )(mask, *pieces, *held)


def pairs_kernel(row, col, factors, last, shifts, places, weights, mhigh, mlow, high, low, *refs):
    count = len(shifts)
    held, outs = refs[:-count], refs[-count:]
    at = places[...]
    pairs, chunk, domv = outs[0].shape
    qs = len(factors)
    size = count * chunk
    blocks = domv // BS
    tiles = domv // LANES
    across = (((1,), (1,)), ((), ()))
    along = (((1,), (0,)), ((), ()))
    dot = functools.partial(lax.dot_general, preferred_element_type=jnp.float32)

    def rows_at(n, p, size):
        return pl.ds(pl.multiple_of(at[0, n * pairs + p], size), size)

    def gather(source, p, q, spans, size):
        first = blocks + col
        sources = [(at[0, (first + 2 * j) * pairs + p], at[0, (first + 2 * j + 1) * pairs + p]) for j in range(tiles)]
        return jnp.concatenate([jnp.concatenate([
            jnp.where(left_of(size), source[a, q, span, :], source[b, q, span, :]) for a, b in sources], 1)
            for span in spans], 0)

    def first_product(p):
        spans = [rows_at(blocks + n, p, chunk) for n in shifts]
        xhigh, xlow = (jnp.concatenate([gather(source, p, q, spans, chunk) for q in factors], 0) for source in (high, low))
        both = dot(jnp.concatenate([xhigh, xlow], 0), mhigh[p], along)
        halfway = both[:qs * size] + both[qs * size:] + dot(xhigh, mlow[p], along)
        return split(jnp.concatenate([halfway[q * size:(q + 1) * size] for q in range(qs)], 1))

    def second_product(p, hhigh, hlow):
        spans = [rows_at(i, p, BS) for i in range(blocks)]
        yhigh, ylow = (jnp.concatenate([gather(source, p, q, spans, BS) for q in factors], 1) for source in (high, low))
        halves = jnp.concatenate([hhigh, hlow], 0)
        if count == 1:
            both = dot(halves, jnp.concatenate([yhigh, ylow], 0), across)
            total = both[:size, :domv] + both[size:, :domv] + (both[:size, domv:] + both[size:, domv:])
        else:
            both = dot(halves, yhigh, across)
            total = both[:size] + both[size:] + dot(hhigh, ylow, across)
        for n, (shift, out) in enumerate(zip(shifts, outs)):
            term = total[n * chunk:(n + 1) * chunk]
            if held:
                term += held[n][p]
            out[p] = term * weights[shift, p] if last else term

    together = pairs if count == 1 else 1
    for start in range(0, pairs, together):
        group = range(start, start + together)
        parts = [first_product(p) for p in group]
        for p, (hhigh, hlow) in zip(group, parts):
            second_product(p, hhigh, hlow)


def contract_pairs(row, col, places, weights, factors, last, shifts, mhigh, mlow, high, low, held=()):
    pairs, domv, _ = mhigh.shape
    chunk = domv // (row * col)
    count = len(shifts)
    return pl.pallas_call(
        functools.partial(pairs_kernel, row, col, factors, last, shifts),
        name="contract_pairs",
        out_shape=[jax.ShapeDtypeStruct((pairs, chunk, domv), jnp.float32)] * count,
        in_specs=[VMEM_SPEC] * (6 + len(held)),
        out_specs=[VMEM_SPEC] * count,
        compiler_params=pltpu.CompilerParams(vmem_limit_bytes=VMEM_LIMIT),
        cost_estimate=pl.CostEstimate(flops=6 * pairs * len(factors) * domv ** 3 * 4 * count // (row * col),
                                      bytes_accessed=8 * high.size, transcendentals=0),
    )(places, weights, mhigh, mlow, high, low, *held)


def add_kernel(*refs):
    total = refs[0][...]
    for ref in refs[1:-1]:
        total += ref[...]
    refs[-1][...] = total


def add_terms(*terms, ahead=0):
    return pl.pallas_call(
        add_kernel,
        name="add_terms",
        out_shape=jax.ShapeDtypeStruct(terms[0].shape, jnp.float32),
        in_specs=[VMEM_SPEC] * len(terms),
        out_specs=VMEM_SPEC,
        compiler_params=pltpu.CompilerParams(vmem_limit_bytes=VMEM_LIMIT),
        cost_estimate=pl.CostEstimate(flops=0, bytes_accessed=ahead + 4 * len(terms) * terms[0].size, transcendentals=0),
    )(*terms)


def body(wide, row, col, amplitudes, factors, domains, domain_mask, block_mask):
    nq, rows, window = factors.shape
    pairs, dom = domains.shape
    z, r, c = lax.axis_index("wide"), lax.axis_index("row"), lax.axis_index("col")
    line = wide if wide == LINE and rows % BS == 0 else 1
    plane = z if line > 1 else 0
    blocks = window // BS
    per_slot = blocks // line
    domv = dom * BS
    tiles = window // LANES
    half = domv // row
    chunk = half // col

    def pick(which, table):
        hits = which[:, None] == jnp.arange(table.shape[0])[None, :]
        return jnp.sum(jnp.where(hits[:, :, None], table[None], 0), axis=1)

    shifts = sorted(range(col), key=lambda s: -bin(s).count("1"))

    blocks_of, flags = domains.T, domain_mask.T
    starts = ((blocks_of // per_slot) ^ plane) * (per_slot * BS) + blocks_of % per_slot * BS
    offsets = r * half + jnp.stack([partner(c, s, col) for s in range(col)]) * chunk
    chosen = pick(offsets // BS, starts) + (offsets % BS)[:, None]
    firsts, seconds = blocks_of[0::2], blocks_of[1::2]
    sources = jnp.stack([firsts % 2 * tiles + firsts // 2, (1 - seconds % 2) * tiles + seconds // 2], 1)
    places = jnp.concatenate([starts, chosen, sources.reshape(-1, pairs)], 0).reshape(1, -1)

    order = jnp.arange(blocks)
    kept = pick(((order // per_slot) ^ plane) * per_slot + order % per_slot, block_mask)
    mask = jnp.repeat(kept, BS, axis=1).astype(jnp.float32)[:, None, :]
    lanes = jnp.repeat(domain_mask, BS, axis=1)
    inner = (domain_mask[:, :, None] * lanes[:, None, :]).astype(jnp.float32)[:, :, None, :]
    outer = (pick(offsets // BS, flags)[:, :, None] * lanes[None]).astype(jnp.float32)[:, :, None, :]

    def siblings(piece):
        return [lax.ppermute(piece, "row", [(i, (i + s) % row) for i in range(row)]) for s in range(1, row)]

    def across(piece, shift):
        return lax.ppermute(piece, "wide", [(i, i ^ shift) for i in range(wide)])

    def others(slot, pieces):
        return [(slot, q + 1, piece) for q, piece in enumerate(pieces)]

    shape = jax.ShapeDtypeStruct((2 * window // LANES, row * nq, window, LANES), jnp.bfloat16)
    prepare = functools.partial(screen, mask)
    mhigh, mlow = mask_amplitudes(inner, amplitudes)
    if line > 1:
        near, cross = across(factors, 1), across(factors, 2)
        high, low = prepare([(0, 0, factors)], shape)
        cross, high, low, mhigh, mlow, places, outer = lax.optimization_barrier(
            (cross, high, low, mhigh, mlow, places, outer))
        last = across(cross, 1)
        early = others(0, siblings(factors)) + [(1, 0, near), (2, 0, cross)]
        s_cross, s_near = siblings(cross), siblings(near)
        high, low = prepare(early, shape, (high, low))
        last, high, low = lax.optimization_barrier((last, high, low))
        contract = functools.partial(contract_pairs, row, col, places, outer)
        s_last = siblings(last)
        high, low = prepare([(3, 0, last)] + others(1, s_near) + others(2, s_cross), shape, (high, low))
        held = contract(range(nq), False, shifts[:1], mhigh, mlow, high, low)
        high, low = prepare(others(3, s_last), shape, (high, low))
        far = contract(range(nq, row * nq), True, shifts[:1], mhigh, mlow, high, low, held)
        far, high, low = lax.optimization_barrier((far, high, low))
        rest = contract(range(row * nq), True, shifts[1:], mhigh, mlow, high, low)
        terms = dict(zip(shifts, far + rest))
    else:
        whole = lax.all_gather(factors, "wide", axis=1, tiled=True)
        high, low = prepare([(0, 0, whole)] + others(0, siblings(whole)), shape)
        contract = functools.partial(contract_pairs, row, col, places, outer)
        rest = contract(range(row * nq), True, shifts, mhigh, mlow, high, low)
        terms = dict(zip(shifts, rest))

    moved = [lax.ppermute(terms[s], "col", [(i, partner(i, s, col)) for i in range(col)]) for s in shifts if s]
    return add_terms(add_terms(terms[0], moved[0], ahead=1 << 24), *moved[1:])


def solution(mesh):
    wide, row, col = (mesh.shape[name] for name in ("wide", "row", "col"))
    return jax.shard_map(
        functools.partial(body, wide, row, col),
        mesh=mesh,
        in_specs=(
            P("wide", None, None),
            P(("row", "col"), "wide", None),
            P("wide", None),
            P("wide", None),
            P(),
        ),
        out_specs=P("wide", ("row", "col"), None),
        check_vma=False,
    )
```

```python
import functools

import jax
import jax.numpy as jnp
from jax import lax
from jax.experimental import pallas as pl
from jax.experimental.pallas import tpu as pltpu
from jax.sharding import PartitionSpec as P

BS = 64
LANES = 128
LINE = 4
VMEM_LIMIT = 40 * 1024 * 1024
VMEM_SPEC = pl.BlockSpec(memory_space=pltpu.VMEM)


def split(value):
    top = value.astype(jnp.bfloat16)
    return top, (value - top.astype(jnp.float32)).astype(jnp.bfloat16)


def partner(r, c, shift, col):
    if col == 4 and shift in (1, 2):
        return c ^ (shift if r % 2 == 0 else 3 - shift)
    if col & (col - 1) == 0:
        return c ^ shift
    return (c + shift) % col


def left_of(rows):
    return lax.broadcasted_iota(jnp.int32, (rows, LANES), 1) < BS


def mask_amplitudes_kernel(weights, amplitudes, high, low):
    pairs, domv, _ = amplitudes.shape
    for p in range(pairs):
        for i in range(domv // BS):
            rows = slice(i * BS, (i + 1) * BS)
            top, rest = split(amplitudes[p, rows, :] * weights[p, i])
            high[p, rows, :] = top
            low[p, rows, :] = rest


def mask_amplitudes(weights, amplitudes):
    shape = jax.ShapeDtypeStruct(amplitudes.shape, jnp.bfloat16)
    return pl.pallas_call(
        mask_amplitudes_kernel,
        name="mask_amplitudes",
        out_shape=[shape] * 2,
        in_specs=[VMEM_SPEC] * 2,
        out_specs=[VMEM_SPEC] * 2,
        compiler_params=pltpu.CompilerParams(vmem_limit_bytes=VMEM_LIMIT),
        cost_estimate=pl.CostEstimate(flops=4 * amplitudes.size, bytes_accessed=8 * amplitudes.size, transcendentals=0),
    )(weights, amplitudes)


def screen_piece(mask, piece, q, slot, high, low):
    nq, rows, window = piece.shape
    tiles = window // LANES
    for h in range(rows // BS):
        block = slot * (rows // BS) + h
        target = slice(block * BS, (block + 1) * BS)
        for t in range(tiles):
            lanes = slice(t * LANES, (t + 1) * LANES)
            for n in range(nq):
                tile = piece[n, h * BS:(h + 1) * BS, lanes] * mask[block, :, lanes]
                for turn, value in ((0, tile), (1, pltpu.roll(tile, BS, 1))):
                    top, rest = split(value)
                    high[turn * tiles + t, q * nq + n, target, :] = top
                    low[turn * tiles + t, q * nq + n, target, :] = rest


def screen_kernel(keys, mask, *refs):
    high, low = refs[-2:]
    for (slot, q), piece in zip(keys, refs):
        screen_piece(mask, piece, q, slot, high, low)


def screen(mask, keyed, shape, held=()):
    keys = [(slot, q) for slot, q, _ in keyed]
    pieces = [piece for _, _, piece in keyed]
    size = sum(piece.size for piece in pieces)
    return pl.pallas_call(
        functools.partial(screen_kernel, keys),
        name="screen_factors",
        out_shape=[shape] * 2,
        in_specs=[VMEM_SPEC] * (1 + len(pieces) + len(held)),
        out_specs=[VMEM_SPEC] * 2,
        input_output_aliases={1 + len(pieces) + i: i for i in range(len(held))},
        compiler_params=pltpu.CompilerParams(vmem_limit_bytes=VMEM_LIMIT),
        cost_estimate=pl.CostEstimate(flops=8 * size, bytes_accessed=12 * size, transcendentals=0),
    )(mask, *pieces, *held)


def pairs_kernel(row, col, factors, last, shifts, places, weights, mhigh, mlow, high, low, *refs):
    count = len(shifts)
    held, outs = refs[:-count], refs[-count:]
    at = places[...]
    pairs, chunk, domv = outs[0].shape
    qs = len(factors)
    size = count * chunk
    blocks = domv // BS
    tiles = domv // LANES
    across = (((1,), (1,)), ((), ()))
    along = (((1,), (0,)), ((), ()))
    dot = functools.partial(lax.dot_general, preferred_element_type=jnp.float32)

    def rows_at(n, p, size):
        return pl.ds(pl.multiple_of(at[0, n * pairs + p], size), size)

    def gather(source, p, q, spans, size):
        first = blocks + col
        sources = [(at[0, (first + 2 * j) * pairs + p], at[0, (first + 2 * j + 1) * pairs + p]) for j in range(tiles)]
        return jnp.concatenate([jnp.concatenate([
            jnp.where(left_of(size), source[a, q, span, :], source[b, q, span, :]) for a, b in sources], 1)
            for span in spans], 0)

    def first_product(p):
        spans = [rows_at(blocks + n, p, chunk) for n in shifts]
        xhigh, xlow = (jnp.concatenate([gather(source, p, q, spans, chunk) for q in factors], 0) for source in (high, low))
        both = dot(jnp.concatenate([xhigh, xlow], 0), mhigh[p], along)
        halfway = both[:qs * size] + both[qs * size:] + dot(xhigh, mlow[p], along)
        return split(jnp.concatenate([halfway[q * size:(q + 1) * size] for q in range(qs)], 1))

    def second_product(p, hhigh, hlow):
        spans = [rows_at(i, p, BS) for i in range(blocks)]
        yhigh, ylow = (jnp.concatenate([gather(source, p, q, spans, BS) for q in factors], 1) for source in (high, low))
        both = dot(jnp.concatenate([hhigh, hlow], 0), yhigh, across)
        total = both[:size] + both[size:] + dot(hhigh, ylow, across)
        for n, (shift, out) in enumerate(zip(shifts, outs)):
            term = total[n * chunk:(n + 1) * chunk]
            if held:
                term += held[n][p]
            out[p] = term * weights[shift, p] if last else term

    together = pairs if count == 1 else 1
    for start in range(0, pairs, together):
        group = range(start, start + together)
        parts = [first_product(p) for p in group]
        for p, (hhigh, hlow) in zip(group, parts):
            second_product(p, hhigh, hlow)


def contract_pairs(row, col, places, weights, factors, last, shifts, mhigh, mlow, high, low, held=()):
    pairs, domv, _ = mhigh.shape
    chunk = domv // (row * col)
    count = len(shifts)
    return pl.pallas_call(
        functools.partial(pairs_kernel, row, col, factors, last, shifts),
        name="contract_pairs",
        out_shape=[jax.ShapeDtypeStruct((pairs, chunk, domv), jnp.float32)] * count,
        in_specs=[VMEM_SPEC] * (6 + len(held)),
        out_specs=[VMEM_SPEC] * count,
        compiler_params=pltpu.CompilerParams(vmem_limit_bytes=VMEM_LIMIT),
        cost_estimate=pl.CostEstimate(flops=6 * pairs * len(factors) * domv ** 3 * 4 * count // (row * col),
                                      bytes_accessed=8 * high.size, transcendentals=0),
    )(places, weights, mhigh, mlow, high, low, *held)


def add_kernel(*refs):
    total = refs[0][...]
    for ref in refs[1:-1]:
        total += ref[...]
    refs[-1][...] = total


def add_terms(*terms, ahead=0):
    return pl.pallas_call(
        add_kernel,
        name="add_terms",
        out_shape=jax.ShapeDtypeStruct(terms[0].shape, jnp.float32),
        in_specs=[VMEM_SPEC] * len(terms),
        out_specs=VMEM_SPEC,
        compiler_params=pltpu.CompilerParams(vmem_limit_bytes=VMEM_LIMIT),
        cost_estimate=pl.CostEstimate(flops=0, bytes_accessed=ahead + 4 * len(terms) * terms[0].size, transcendentals=0),
    )(*terms)


def body(wide, row, col, amplitudes, factors, domains, domain_mask, block_mask):
    nq, rows, window = factors.shape
    pairs, dom = domains.shape
    z, r, c = lax.axis_index("wide"), lax.axis_index("row"), lax.axis_index("col")
    line = wide if wide == LINE and rows % BS == 0 else 1
    plane = z if line > 1 else 0
    blocks = window // BS
    per_slot = blocks // line
    domv = dom * BS
    tiles = window // LANES
    half = domv // row
    chunk = half // col

    def pick(which, table):
        hits = which[:, None] == jnp.arange(table.shape[0])[None, :]
        return jnp.sum(jnp.where(hits[:, :, None], table[None], 0), axis=1)

    shifts = sorted(range(col), key=lambda s: -bin(s).count("1"))

    blocks_of, flags = domains.T, domain_mask.T
    starts = ((blocks_of // per_slot) ^ plane) * (per_slot * BS) + blocks_of % per_slot * BS
    offsets = r * half + jnp.stack([jnp.where(r % 2 == 0, partner(0, c, s, col), partner(1, c, s, col)) for s in range(col)]) * chunk
    chosen = pick(offsets // BS, starts) + (offsets % BS)[:, None]
    firsts, seconds = blocks_of[0::2], blocks_of[1::2]
    sources = jnp.stack([firsts % 2 * tiles + firsts // 2, (1 - seconds % 2) * tiles + seconds // 2], 1)
    places = jnp.concatenate([starts, chosen, sources.reshape(-1, pairs)], 0).reshape(1, -1)

    order = jnp.arange(blocks)
    kept = pick(((order // per_slot) ^ plane) * per_slot + order % per_slot, block_mask)
    mask = jnp.repeat(kept, BS, axis=1).astype(jnp.float32)[:, None, :]
    lanes = jnp.repeat(domain_mask, BS, axis=1)
    inner = (domain_mask[:, :, None] * lanes[:, None, :]).astype(jnp.float32)[:, :, None, :]
    outer = (pick(offsets // BS, flags)[:, :, None] * lanes[None]).astype(jnp.float32)[:, :, None, :]

    def siblings(piece):
        return [lax.ppermute(piece, "row", [(i, (i + s) % row) for i in range(row)]) for s in range(1, row)]

    def across(piece, shift):
        return lax.ppermute(piece, "wide", [(i, i ^ shift) for i in range(wide)])

    def others(slot, pieces):
        return [(slot, q + 1, piece) for q, piece in enumerate(pieces)]

    shape = jax.ShapeDtypeStruct((2 * window // LANES, row * nq, window, LANES), jnp.bfloat16)
    prepare = functools.partial(screen, mask)
    mhigh, mlow = mask_amplitudes(inner, amplitudes)
    if line > 1:
        near, cross = across(factors, 1), across(factors, 2)
        high, low = prepare([(0, 0, factors)], shape)
        cross, high, low, mhigh, mlow, places, outer = lax.optimization_barrier(
            (cross, high, low, mhigh, mlow, places, outer))
        last = across(cross, 1)
        early = others(0, siblings(factors)) + [(1, 0, near), (2, 0, cross)]
        s_cross, s_near = siblings(cross), siblings(near)
        high, low = prepare(early, shape, (high, low))
        last, high, low = lax.optimization_barrier((last, high, low))
        contract = functools.partial(contract_pairs, row, col, places, outer)
        s_last = siblings(last)
        high, low = prepare([(3, 0, last)] + others(1, s_near) + others(2, s_cross), shape, (high, low))
        held = contract(range(nq), False, shifts[:1], mhigh, mlow, high, low)
        high, low = prepare(others(3, s_last), shape, (high, low))
        far = contract(range(nq, row * nq), True, shifts[:1], mhigh, mlow, high, low, held)
        far, high, low = lax.optimization_barrier((far, high, low))
        rest = contract(range(row * nq), True, shifts[1:], mhigh, mlow, high, low)
        terms = dict(zip(shifts, far + rest))
    else:
        whole = lax.all_gather(factors, "wide", axis=1, tiled=True)
        high, low = prepare([(0, 0, whole)] + others(0, siblings(whole)), shape)
        contract = functools.partial(contract_pairs, row, col, places, outer)
        rest = contract(range(row * nq), True, shifts, mhigh, mlow, high, low)
        terms = dict(zip(shifts, rest))

    moved = [lax.ppermute(terms[s], ("row", "col"), [(i * col + k, i * col + partner(i, k, s, col)) for i in range(row) for k in range(col)])
             for s in shifts if s]
    return add_terms(add_terms(terms[0], moved[0], ahead=1 << 24), *moved[1:])


def solution(mesh):
    wide, row, col = (mesh.shape[name] for name in ("wide", "row", "col"))
    return jax.shard_map(
        functools.partial(body, wide, row, col),
        mesh=mesh,
        in_specs=(
            P("wide", None, None),
            P(("row", "col"), "wide", None),
            P("wide", None),
            P("wide", None),
            P(),
        ),
        out_specs=P("wide", ("row", "col"), None),
        check_vma=False,
    )
```
